32 devices in a mesh: grp: 2 (over y), ma: 4 (over z), freq: 2 (over x), bl: 2 (over core).
Axes of the slice: x: 2, y: 2, z: 4, core: 2. Of those that a mesh axis runs over, the one named last changes fastest.
Arguments:
- sky_modes: bfloat16 [32, 2, 128, 512], P('ma', None, 'grp'), parts along dimension 2, may hold values from -6 to 6
- beam_modes: bfloat16 [32, 2, 16, 512], P('ma'), may hold values from -0.25 to 0.25
- visibilities: bfloat16 [32, 32, 2, 128, 512], P('freq', 'ma', None, 'grp', 'bl'), parts along dimension 3, may hold values from -6 to 6
- fringe: float32 [32, 2, 512], P('freq', None, 'bl'), may hold values from -4 to 4
- noise_weight: float32 [32, 512], P('freq', 'bl'), may hold values from 0.0007 to 0.006
- feed_map: int32 [512], P('bl'), may hold values from 0 to 15
Outputs:
- beam_grad: float32 [32, 2, 32, 512], P('ma', None, 'grp', 'freq'), parts along dimension 2
The draws below stay inside these ranges and needn't reach their ends.
There are 2 independent parts, one for each index of `grp`. The reference program is written for one: setup_inputs(seed, part) draws one part's arguments, and reference() takes and returns one part's arrays. A program takes and returns all parts, laid end to end along the dimension named above; an argument that names none is the same for every part. Nothing has to cross between parts.
All inputs are finite; a program needn't handle non-finite values.
Results may differ from the reference program's by a relative error of at most 0.00075.
Values may be sent and summed in bfloat16 or wider, within the bound.
No kernel may reach another device: no remote copies, remote signals or barrier semaphores. Data moves between devices by JAX's collectives and lax.ppermute only.
A program may use at most 64 MiB of HBM per device.

```python
import math
import jax
import jax.numpy as jnp
from jax import lax

S = 64
CH = 32
NB = 512
NQ = 16
L = 512
M = 32


def with_ends(drawn, key, smallest, top_value):
    extent = drawn.shape
    place = [jax.random.randint(jax.random.fold_in(key, axis), (), 0, extent[axis]) for axis in range(len(extent))]
    drawn = drawn.at[tuple(place)].set(smallest)
    longest = extent.index(max(extent))
    place[longest] = (place[longest] + 1) % extent[longest]
    return drawn.at[tuple(place)].set(top_value)


def shard_levels(key, extent, split, smallest, largest):
    gain, own = 1.0, jax.random.fold_in(key, 6)
    for position, parts in split:
        draws = jnp.exp(jax.random.uniform(jax.random.fold_in(own, position), (parts,), jnp.float32, smallest / len(split), largest / len(split)))
        gain = gain * jnp.repeat(draws, extent[position] // parts).reshape([-1 if axis == position else 1 for axis in range(len(extent))])
    return gain


def scatter_about(key, dims, deviation, most, split=(), kind=jnp.bfloat16):
    gain = shard_levels(key, dims, split, -0.22, 0.18) if split else 1.0
    entries = jax.random.normal(key, dims, jnp.float32) * deviation * gain
    return jnp.minimum(jnp.maximum(entries, -most), most).astype(kind)


def setup_inputs(seed: int = 0, part: int = 0) -> dict:
    arg_keys = jax.random.split(jax.random.key(seed), 7)
    part_splits = jax.random.split(jax.random.fold_in(arg_keys[6], part), 7)
    sky_modes = scatter_about(part_splits[0], (M, 2, S, L), 1.0, 6.0, ((0, 4),))
    beam_modes = scatter_about(arg_keys[1], (M, 2, NQ, L), L ** -0.5, 0.25, ((0, 4),))
    visibilities = scatter_about(part_splits[2], (CH, M, 2, S, NB), 1.0, 6.0, ((0, 2), (1, 4), (4, 2)))
    fringe = scatter_about(arg_keys[3], (CH, 2, NB), 0.7, 4.0, ((0, 2), (2, 2)), jnp.float32)
    noise_weight = jnp.clip(jnp.exp(math.log(0.006) - 2.1484345 * jax.random.uniform(arg_keys[4], (CH, NB), jnp.float32) ** shard_levels(arg_keys[4], (CH, NB), ((0, 2), (1, 2)), -0.2, 0.2)), 0.0007, 0.006)
    feed_map = with_ends(jax.random.randint(arg_keys[5], (NB,), 0, NQ), jax.random.fold_in(arg_keys[5], 1), 0, NQ - 1).astype(jnp.int32)
    return {"sky_modes": sky_modes, "beam_modes": beam_modes, "visibilities": visibilities, "fringe": fringe, "noise_weight": noise_weight, "feed_map": feed_map}


def pair_product(pattern, a_re, a_im, b_re, b_im):
    def single(left_side, right_side):
        return jnp.einsum(pattern, left_side, right_side, precision=lax.Precision.HIGHEST)
    return single(a_re, b_re) - single(a_im, b_im), single(a_re, b_im) + single(a_im, b_re)


def reference(sky_modes, beam_modes, visibilities, fringe, noise_weight, feed_map):
    total = sky_modes.shape[0]
    slots = jnp.arange(total, dtype=jnp.int32)
    mirror_index = ((total - slots) % total).astype(jnp.int32)
    sky_mirror = sky_modes[mirror_index]
    parity = jnp.where(slots % 2 == 0, 1.0, -1.0).astype(jnp.float32)
    classes = beam_modes.shape[2]
    onehot = (feed_map[None, :] == jnp.arange(classes, dtype=jnp.int32)[:, None]).astype(jnp.float32)
    fringe_re = fringe[:, 0][:, None, :]
    fringe_im = fringe[:, 1][:, None, :]
    weight = noise_weight[:, None, :]

    def per_slot(slot):
        nearby = lax.dynamic_index_in_dim(sky_modes, slot, 0, keepdims=False).astype(jnp.float32)
        distant = lax.dynamic_index_in_dim(sky_mirror, slot, 0, keepdims=False).astype(jnp.float32)
        beams = lax.dynamic_index_in_dim(beam_modes, slot, 0, keepdims=False).astype(jnp.float32)
        observed = lax.dynamic_index_in_dim(visibilities, slot, 1, keepdims=False).astype(jnp.float32)
        sign = lax.dynamic_index_in_dim(parity, slot, 0, keepdims=False)
        direct = pair_product("ql,sl->qs", beams[0], beams[1], nearby[0], nearby[1])
        crossed = pair_product("ql,sl->qs", beams[0], beams[1], distant[0], -distant[1])
        resp_re = 0.5 * (direct[0] + sign * crossed[0])
        resp_im = 0.5 * (direct[1] + sign * crossed[1])
        spread_re = jnp.take(resp_re, feed_map, axis=0).T[None]
        spread_im = jnp.take(resp_im, feed_map, axis=0).T[None]
        model_re = fringe_re * spread_re - fringe_im * spread_im
        model_im = fringe_re * spread_im + fringe_im * spread_re
        resid_re = weight * (model_re - observed[:, 0])
        resid_im = weight * (model_im - observed[:, 1])
        weighted_re = lax.optimization_barrier((fringe_re * resid_re + fringe_im * resid_im).astype(jnp.bfloat16))
        weighted_im = lax.optimization_barrier((fringe_re * resid_im - fringe_im * resid_re).astype(jnp.bfloat16))
        pooled_re = jnp.einsum("fsb,qb->qs", weighted_re.astype(jnp.float32), onehot, precision=lax.Precision.HIGHEST)
        pooled_im = jnp.einsum("fsb,qb->qs", weighted_im.astype(jnp.float32), onehot, precision=lax.Precision.HIGHEST)
        own_re, own_im = pair_product("qs,sl->ql", pooled_re, pooled_im, nearby[0], -nearby[1])
        far_re, far_im = pair_product("qs,sl->ql", pooled_re, pooled_im, distant[0], distant[1])
        return jnp.stack([0.5 * (own_re + sign * far_re), 0.5 * (own_im + sign * far_im)])

    return lax.map(per_slot, slots)
```

```python
import functools

import jax
import jax.numpy as jnp
from jax import lax
from jax.experimental import pallas as pl
from jax.experimental.pallas import tpu as pltpu
from jax.sharding import PartitionSpec as P

BF = jnp.bfloat16
F32 = jnp.float32
NT = (((1,), (1,)), ((), ()))
NN = (((1,), (0,)), ((), ()))


def split3(x):
    top = x.astype(BF)
    rest = x - top.astype(F32)
    mid = rest.astype(BF)
    return top, mid, (rest - mid.astype(F32)).astype(BF)


def dot(a, b, dims):
    return lax.dot_general(a, b, dims, preferred_element_type=F32)


def my_place():
    return lax.axis_index("freq") * lax.axis_size("bl") + lax.axis_index("bl")


def pool_kernel(devices, classes, vis, fringe, noise, feeds, *refs):
    outs, (buf, ready, sems) = refs[:devices], refs[devices:]
    channels, slots, _, skies, lines = vis.shape
    copies = [pltpu.make_async_copy(vis.at[f], buf.at[f], sems.at[f]) for f in range(channels)]
    for copy in copies:
        copy.start()
    onehot = lax.broadcasted_iota(jnp.int32, (classes, lines), 0) == feeds[...]
    weight = noise[...]
    real = fringe[:, 0, :]
    imag = fringe[:, 1, :]
    gain = jnp.sum(weight * (real * real + imag * imag), axis=0, keepdims=True)
    gain = jnp.sum(jnp.where(onehot, gain, 0.0), axis=1, keepdims=True)
    parts_re = [p.astype(F32) for p in split3(weight * real)]
    parts_im = [p.astype(F32) for p in split3(-weight * imag)]

    def spread(part, f):
        return jnp.where(onehot, part[f : f + 1, :], 0.0)

    total = None
    for f in range(channels):
        rows_re = [spread(p, f) for p in parts_re]
        rows_im = [spread(p, f) for p in parts_im]
        left_re = jnp.concatenate([y for x in zip(rows_re, rows_im) for y in x], 0).astype(BF)
        left_im = jnp.concatenate([y for x in zip(rows_im, rows_re) for y in (-x[0], x[1])], 0).astype(BF)
        copies[f].wait()
        for part, left in ((0, left_re), (1, left_im)):
            term = dot(left, buf[f, :, part].reshape(slots * skies, lines), NT)
            total = term if total is None else total + term
    wide = 2 * classes
    total = total[:wide] + total[wide : 2 * wide] + total[2 * wide :]
    width = slots * skies // devices
    for d in range(devices):
        ready[d, :wide] = total[:, d * width : (d + 1) * width]
        ready[d, wide:] = jnp.broadcast_to(gain, (classes, width))
    place = my_place()
    for r in range(devices):
        outs[r][...] = ready[place ^ r]


def pool(vis, fringe, noise, feeds, devices, classes):
    channels, slots, _, skies, lines = vis.shape
    width = slots * skies // devices
    vmem = pl.BlockSpec(memory_space=pltpu.VMEM)
    return pl.pallas_call(
        functools.partial(pool_kernel, devices, classes),
        in_specs=[pl.BlockSpec(memory_space=pl.ANY), vmem, vmem, vmem],
        out_specs=[vmem] * devices,
        out_shape=[jax.ShapeDtypeStruct((3 * classes, width), F32)] * devices,
        scratch_shapes=[
            pltpu.VMEM(vis.shape, BF),
            pltpu.VMEM((devices, 3 * classes, width), F32),
            pltpu.SemaphoreType.DMA((channels,)),
        ],
        compiler_params=pltpu.CompilerParams(vmem_limit_bytes=48 << 20),
        cost_estimate=pl.CostEstimate(
            flops=2 * 6 * classes * vis.size, bytes_accessed=2 * vis.size, transcendentals=0
        ),
    )(vis, fringe, noise, feeds.reshape(1, lines))


def grad_kernel(devices, each, place, *refs):
    sky, beam = refs[:2]
    far = refs[2 : 2 + each]
    pooled = refs[2 + each : 2 + each + devices]
    outs = refs[2 + each + devices : -1]
    whole = refs[-1]
    _, _, skies, degrees = sky.shape
    classes = beam.shape[2]
    wide = 2 * classes
    sums = pooled[0][...]
    for ref in pooled[1:]:
        sums = sums + ref[...]
    gain = 0.5 * sums[wide:]
    for i in range(each):
        parity = jnp.where((place[0] * each + i) % 2 == 0, 1.0, -1.0).astype(F32)
        mine, other = sky[i], far[i][0]
        b_re, b_im = beam[i, 0].astype(F32), beam[i, 1].astype(F32)
        at = slice(i * skies, (i + 1) * skies)

        def rows(a, b):
            return jnp.concatenate([a, b], 0).astype(BF)

        resp = dot(rows(b_re, b_im), mine[0], NT) + dot(rows(-b_im, b_re), mine[1], NT)
        resp += parity * (dot(rows(b_re, b_im), other[0], NT) + dot(rows(b_im, -b_re), other[1], NT))
        scale = gain[:, at]
        p_re = 0.5 * (scale * resp[:classes] - sums[:classes, at])
        p_im = 0.5 * (scale * resp[classes:] - sums[classes:wide, at])
        near = jnp.concatenate([jnp.concatenate([p_re, p_im], 1), jnp.concatenate([p_im, -p_re], 1)], 0)
        away = parity * jnp.concatenate([jnp.concatenate([p_re, -p_im], 1), jnp.concatenate([p_im, p_re], 1)], 0)
        near = jnp.concatenate(split3(near), 0)
        away = jnp.concatenate(split3(away), 0)
        grad = dot(near, mine.reshape(2 * skies, degrees), NN) + dot(away, other.reshape(2 * skies, degrees), NN)
        grad = grad[:wide] + grad[wide : 2 * wide] + grad[2 * wide :]
        step = degrees // len(outs)
        for h in range(len(outs)):
            whole[h, i] = grad[:, h * step : (h + 1) * step]
    row = lax.axis_index("freq")
    for h in range(len(outs)):
        outs[h][...] = whole[row ^ h]


def gradient(sky, beam, far, pooled, devices, rows):
    slots, _, skies, degrees = sky.shape
    classes = beam.shape[2]
    each = slots // devices
    vmem = pl.BlockSpec(memory_space=pltpu.VMEM)
    shape = (each, 2 * classes, degrees // rows)
    out_spec = pl.BlockSpec(shape, lambda i, place: (0, 0, 0))
    return pl.pallas_call(
        functools.partial(grad_kernel, devices, each),
        grid_spec=pltpu.PrefetchScalarGridSpec(
            num_scalar_prefetch=1,
            grid=(1,),
            in_specs=[
                pl.BlockSpec((each, 2, skies, degrees), lambda i, place: (place[0], 0, 0, 0)),
                pl.BlockSpec((each, 2, classes, degrees), lambda i, place: (place[0], 0, 0, 0)),
                *[pl.BlockSpec(x.shape, lambda i, place: (0, 0, 0, 0)) for x in far],
                *[pl.BlockSpec(x.shape, lambda i, place: (0, 0)) for x in pooled],
            ],
            out_specs=[out_spec] * rows,
            scratch_shapes=[pltpu.VMEM((rows, *shape), F32)],
        ),
        out_shape=[jax.ShapeDtypeStruct(shape, F32)] * rows,
    )(my_place().astype(jnp.int32).reshape(1), sky, beam, *far, *pooled)


def join_kernel(each, *refs):
    pieces, out = refs[:-1], refs[-1]
    place = my_place()
    for r, piece in enumerate(pieces):
        out[pl.ds((place ^ r) * each, each)] = piece[...]


def join(pieces):
    each, rows, step = pieces[0].shape
    vmem = pl.BlockSpec(memory_space=pltpu.VMEM)
    return pl.pallas_call(
        functools.partial(join_kernel, each),
        in_specs=[vmem] * len(pieces),
        out_specs=vmem,
        out_shape=jax.ShapeDtypeStruct((each * len(pieces), rows, step), F32),
    )(*pieces)


def body(sky, beam, vis, fringe, noise, feeds):
    slots = sky.shape[0]
    classes = beam.shape[2]
    blocks, rows, cores = (lax.axis_size(x) for x in ("ma", "freq", "bl"))
    devices = rows * cores
    each = slots // devices
    place = my_place()

    far = []
    for i in range(each):
        sent = lax.dynamic_slice_in_dim(sky, (slots - (place * each + i)) % slots, 1, 0)
        pairs = []
        for a in range(blocks):
            for c in range(devices):
                to = (blocks - a) % blocks if c * each + i == 0 else blocks - 1 - a
                pairs.append((a * devices + c, to * devices + c))
        far.append(lax.ppermute(sent, ("ma", "freq", "bl"), pairs))

    def across(x, r):
        return lax.ppermute(x, ("freq", "bl"), [(c, c ^ r) for c in range(devices)]) if r else x

    pooled = pool(vis, fringe, noise, feeds, devices, classes)
    pooled = [across(x, r) for r, x in enumerate(pooled)]
    blocks_out = gradient(sky, beam, far, pooled, devices, rows)
    pieces = [across(blocks_out[r // cores], r) for r in range(devices)]
    out = join(pieces)
    return out.reshape(slots, 2, classes, out.shape[-1])


def solution(mesh):
    in_specs = (
        P("ma", None, "grp", None),
        P("ma", None, None, None),
        P("freq", "ma", None, "grp", "bl"),
        P("freq", None, "bl"),
        P("freq", "bl"),
        P("bl"),
    )
    out_specs = P("ma", None, "grp", "freq")
    return jax.shard_map(body, mesh=mesh, in_specs=in_specs, out_specs=out_specs, check_vma=False)
```

```python
import functools

import jax
import jax.numpy as jnp
from jax import lax
from jax.experimental import pallas as pl
from jax.experimental.pallas import tpu as pltpu
from jax.sharding import PartitionSpec as P

BF = jnp.bfloat16
F32 = jnp.float32
AHEAD = 6
NT = (((1,), (1,)), ((), ()))
NN = (((1,), (0,)), ((), ()))


def split3(x):
    top = x.astype(BF)
    rest = x - top.astype(F32)
    mid = rest.astype(BF)
    return top, mid, (rest - mid.astype(F32)).astype(BF)


def dot(a, b, dims):
    return lax.dot_general(a, b, dims, preferred_element_type=F32)


def my_place():
    return lax.axis_index("freq") * lax.axis_size("bl") + lax.axis_index("bl")


def rows(a, b):
    return jnp.concatenate([a, b], 0).astype(BF)


def pool_kernel(devices, classes, vis, fringe, noise, feeds, *refs):
    outs = refs[:devices]
    buf, fringe_v, noise_v, feeds_v, ready, sems, small = refs[devices:]
    channels, slots, _, skies, lines = vis.shape
    ahead = min(AHEAD, channels)
    little = [
        pltpu.make_async_copy(src, dst, small.at[i])
        for i, (src, dst) in enumerate([(feeds, feeds_v), (fringe, fringe_v), (noise, noise_v)])
    ]
    copies = [pltpu.make_async_copy(vis.at[f], buf.at[f], sems.at[f]) for f in range(channels)]
    for copy in little + copies[:ahead]:
        copy.start()
    for copy in little:
        copy.wait()
    onehot = lax.broadcasted_iota(jnp.int32, (classes, lines), 0) == feeds_v[...]
    weight = noise_v[...]
    real = fringe_v[:, 0, :]
    imag = fringe_v[:, 1, :]
    gain = jnp.sum(weight * (real * real + imag * imag), axis=0, keepdims=True)
    gain = jnp.sum(jnp.where(onehot, gain, 0.0), axis=1, keepdims=True)
    parts_re = [p.astype(F32) for p in split3(weight * real)]
    parts_im = [p.astype(F32) for p in split3(-weight * imag)]

    def spread(part, f):
        return jnp.where(onehot, part[f : f + 1, :], 0.0)

    total = None
    for f in range(channels):
        rows_re = [spread(p, f) for p in parts_re]
        rows_im = [spread(p, f) for p in parts_im]
        left_re = jnp.concatenate([y for x in zip(rows_re, rows_im) for y in x], 0).astype(BF)
        left_im = jnp.concatenate([y for x in zip(rows_im, rows_re) for y in (-x[0], x[1])], 0).astype(BF)
        copies[f].wait()
        if f + ahead < channels:
            copies[f + ahead].start()
        for part, left in ((0, left_re), (1, left_im)):
            term = dot(left, buf[f, :, part].reshape(slots * skies, lines), NT)
            total = term if total is None else total + term
    wide = 2 * classes
    total = total[:wide] + total[wide : 2 * wide] + total[2 * wide :]
    width = slots * skies // devices
    for d in range(devices):
        ready[d, :wide] = total[:, d * width : (d + 1) * width]
        ready[d, wide:] = jnp.broadcast_to(gain, (classes, width))
    place = my_place()
    for r in range(devices):
        outs[r][...] = ready[place ^ r]


def pool(vis, fringe, noise, feeds, devices, classes):
    channels, slots, _, skies, lines = vis.shape
    width = slots * skies // devices
    vmem = pl.BlockSpec(memory_space=pltpu.VMEM)
    feeds = feeds.reshape(1, lines)
    return pl.pallas_call(
        functools.partial(pool_kernel, devices, classes),
        in_specs=[pl.BlockSpec(memory_space=pl.ANY)] * 4,
        out_specs=[vmem] * devices,
        out_shape=[jax.ShapeDtypeStruct((3 * classes, width), F32)] * devices,
        scratch_shapes=[
            pltpu.VMEM(vis.shape, BF),
            pltpu.VMEM(fringe.shape, F32),
            pltpu.VMEM(noise.shape, F32),
            pltpu.VMEM(feeds.shape, jnp.int32),
            pltpu.VMEM((devices, 3 * classes, width), F32),
            pltpu.SemaphoreType.DMA((channels,)),
            pltpu.SemaphoreType.DMA((3,)),
        ],
        compiler_params=pltpu.CompilerParams(vmem_limit_bytes=60 << 20),
        cost_estimate=pl.CostEstimate(
            flops=2 * 6 * classes * vis.size, bytes_accessed=2 * vis.size, transcendentals=0
        ),
    )(vis, fringe, noise, feeds)


def near_kernel(sky, beam, *outs):
    for i, out in enumerate(outs):
        b_re, b_im = beam[i, 0].astype(F32), beam[i, 1].astype(F32)
        out[...] = dot(rows(b_re, b_im), sky[i, 0], NT) + dot(rows(-b_im, b_re), sky[i, 1], NT)


def near(sky, beam):
    each, _, skies, _ = sky.shape
    vmem = pl.BlockSpec(memory_space=pltpu.VMEM)
    return pl.pallas_call(
        near_kernel,
        in_specs=[vmem] * 2,
        out_specs=[vmem] * each,
        out_shape=[jax.ShapeDtypeStruct((2 * beam.shape[2], skies), F32)] * each,
        compiler_params=pltpu.CompilerParams(vmem_limit_bytes=8 << 20),
        cost_estimate=pl.CostEstimate(flops=1000, bytes_accessed=1000, transcendentals=0),
    )(sky, beam)


def grad_kernel(cuts, sky, beam, *refs):
    each, _, skies, degrees = sky.shape
    direct, far, pooled = refs[:each], refs[each : 2 * each], refs[2 * each : -cuts - 1]
    outs, whole = refs[-cuts - 1 : -1], refs[-1]
    classes = beam.shape[2]
    wide = 2 * classes
    step = degrees // cuts
    place = my_place()
    sums = pooled[0][...]
    for ref in pooled[1:]:
        sums = sums + ref[...]
    gain = 0.5 * sums[wide:]
    for i in range(each):
        at = slice(i * skies, (i + 1) * skies)
        parity = jnp.where((place * each + i) % 2 == 0, 1.0, -1.0).astype(F32)
        mine, other = sky[i], far[i][0]
        b_re, b_im = beam[i, 0].astype(F32), beam[i, 1].astype(F32)
        crossed = dot(rows(b_re, b_im), other[0], NT) + dot(rows(b_im, -b_re), other[1], NT)
        resp = direct[i][...] + parity * crossed
        p_re = 0.5 * (gain[:, at] * resp[:classes] - sums[:classes, at])
        p_im = 0.5 * (gain[:, at] * resp[classes:] - sums[classes:wide, at])
        own = jnp.concatenate([jnp.concatenate([p_re, p_im], 1), jnp.concatenate([p_im, -p_re], 1)], 0)
        away = parity * jnp.concatenate([jnp.concatenate([p_re, -p_im], 1), jnp.concatenate([p_im, p_re], 1)], 0)
        own = jnp.concatenate(split3(own), 0)
        away = jnp.concatenate(split3(away), 0)
        grad = dot(own, mine.reshape(2 * skies, degrees), NN) + dot(away, other.reshape(2 * skies, degrees), NN)
        grad = grad[:wide] + grad[wide : 2 * wide] + grad[2 * wide :]
        for h in range(cuts):
            whole[h, i] = grad[:, h * step : (h + 1) * step]
    row = lax.axis_index("freq")
    for h in range(cuts):
        outs[h][...] = whole[row ^ h]


def gradient(cuts, sky, beam, direct, far, pooled):
    each = sky.shape[0]
    classes, degrees = beam.shape[2:]
    vmem = pl.BlockSpec(memory_space=pltpu.VMEM)
    shape = (each, 2 * classes, degrees // cuts)
    return pl.pallas_call(
        functools.partial(grad_kernel, cuts),
        in_specs=[vmem] * (2 + 2 * each + len(pooled)),
        out_specs=[vmem] * cuts,
        out_shape=[jax.ShapeDtypeStruct(shape, F32)] * cuts,
        scratch_shapes=[pltpu.VMEM((cuts, *shape), F32)],
        compiler_params=pltpu.CompilerParams(vmem_limit_bytes=8 << 20),
    )(sky, beam, *direct, *far, *pooled)


def join_kernel(*refs):
    pieces, out = refs[:-1], refs[-1]
    each = pieces[0].shape[0]
    place = my_place()
    for r, piece in enumerate(pieces):
        out[pl.ds((place ^ r) * each, each)] = piece[...]


def join(pieces):
    each, wide, step = pieces[0].shape
    vmem = pl.BlockSpec(memory_space=pltpu.VMEM)
    return pl.pallas_call(
        join_kernel,
        in_specs=[vmem] * len(pieces),
        out_specs=vmem,
        out_shape=jax.ShapeDtypeStruct((each * len(pieces), wide, step), F32),
        compiler_params=pltpu.CompilerParams(vmem_limit_bytes=8 << 20),
    )(*pieces)


def body(sky, beam, vis, fringe, noise, feeds):
    slots = sky.shape[0]
    classes = beam.shape[2]
    blocks, cuts, cores = (lax.axis_size(x) for x in ("ma", "freq", "bl"))
    devices = cuts * cores
    each = slots // devices
    place = my_place()

    def across(x, r):
        return lax.ppermute(x, ("freq", "bl"), [(c, c ^ r) for c in range(devices)]) if r else x

    def mirror_of(i, sky):
        return lax.dynamic_slice_in_dim(sky, (slots - (place * each + i)) % slots, 1, 0)

    def mirrored(i, sent):
        pairs = []
        for a in range(blocks):
            for c in range(devices):
                to = (blocks - a) % blocks if c * each + i == 0 else blocks - 1 - a
                pairs.append((a * devices + c, to * devices + c))
        return lax.ppermute(sent, ("ma", "freq", "bl"), pairs)

    last = each - 1
    sent = mirror_of(last, sky)
    far = [None] * last + [mirrored(last, sent)]
    vis, _ = lax.optimization_barrier((vis, sent))
    sums = pool(vis, fringe, noise, feeds, devices, classes)
    *sums, later, later_beam = lax.optimization_barrier((*sums, sky, beam))
    for i in range(last):
        sent = mirror_of(i, later)
        far[i] = mirrored(i, sent)
        *sums, later, later_beam, _ = lax.optimization_barrier((*sums, later, later_beam, sent))
    pooled = [across(x, r) for r, x in enumerate(sums)]
    own = lax.dynamic_slice_in_dim(later, place * each, each, 0)
    own_beam = lax.dynamic_slice_in_dim(later_beam, place * each, each, 0)
    direct = near(own, own_beam)
    cut = gradient(cuts, own, own_beam, direct, far, pooled)
    cut = [across(x, h * cores) for h, x in enumerate(cut)]
    pieces = [across(x, r) for x in cut for r in range(cores)]
    out = join(pieces)
    return out.reshape(slots, 2, classes, out.shape[-1])


def solution(mesh):
    in_specs = (
        P("ma", None, "grp", None),
        P("ma", None, None, None),
        P("freq", "ma", None, "grp", "bl"),
        P("freq", None, "bl"),
        P("freq", "bl"),
        P("bl"),
    )
    out_specs = P("ma", None, "grp", "freq")
    return jax.shard_map(body, mesh=mesh, in_specs=in_specs, out_specs=out_specs, check_vma=False)
```

```python
import functools

import jax
import jax.numpy as jnp
from jax import lax
from jax.experimental import pallas as pl
from jax.experimental.pallas import tpu as pltpu
from jax.sharding import PartitionSpec as P

BF = jnp.bfloat16
F32 = jnp.float32
AHEAD = 6
NT = (((1,), (1,)), ((), ()))
NN = (((1,), (0,)), ((), ()))


def split3(x):
    top = x.astype(BF)
    rest = x - top.astype(F32)
    mid = rest.astype(BF)
    return top, mid, (rest - mid.astype(F32)).astype(BF)


def dot(a, b, dims):
    return lax.dot_general(a, b, dims, preferred_element_type=F32)


def my_place():
    return lax.axis_index("freq") * lax.axis_size("bl") + lax.axis_index("bl")


def rows(a, b):
    return jnp.concatenate([a, b], 0).astype(BF)


def pool_kernel(devices, classes, vis, fringe, noise, feeds, *refs):
    outs = refs[:devices]
    buf, fringe_v, noise_v, feeds_v, ready, sems, small = refs[devices:]
    channels, slots, _, skies, lines = vis.shape
    ahead = min(AHEAD, channels)
    little = [
        pltpu.make_async_copy(src, dst, small.at[i])
        for i, (src, dst) in enumerate([(feeds, feeds_v), (fringe, fringe_v), (noise, noise_v)])
    ]
    copies = [pltpu.make_async_copy(vis.at[f], buf.at[f], sems.at[f]) for f in range(channels)]
    for copy in little + copies[:ahead]:
        copy.start()
    for copy in little:
        copy.wait()
    onehot = lax.broadcasted_iota(jnp.int32, (classes, lines), 0) == feeds_v[...]
    weight = noise_v[...]
    real = fringe_v[:, 0, :]
    imag = fringe_v[:, 1, :]
    gain = jnp.sum(weight * (real * real + imag * imag), axis=0, keepdims=True)
    gain = jnp.sum(jnp.where(onehot, gain, 0.0), axis=1, keepdims=True)
    parts_re = [p.astype(F32) for p in split3(weight * real)]
    parts_im = [p.astype(F32) for p in split3(-weight * imag)]

    def spread(part, f):
        return jnp.where(onehot, part[f : f + 1, :], 0.0)

    total = None
    for f in range(channels):
        rows_re = [spread(p, f) for p in parts_re]
        rows_im = [spread(p, f) for p in parts_im]
        left_re = jnp.concatenate([y for x in zip(rows_re, rows_im) for y in x], 0).astype(BF)
        left_im = jnp.concatenate([y for x in zip(rows_im, rows_re) for y in (-x[0], x[1])], 0).astype(BF)
        copies[f].wait()
        if f + ahead < channels:
            copies[f + ahead].start()
        for part, left in ((0, left_re), (1, left_im)):
            term = dot(left, buf[f, :, part].reshape(slots * skies, lines), NT)
            total = term if total is None else total + term
    wide = 2 * classes
    total = total[:wide] + total[wide : 2 * wide] + total[2 * wide :]
    width = slots * skies // devices
    for d in range(devices):
        ready[d, :wide] = total[:, d * width : (d + 1) * width]
        ready[d, wide:] = jnp.broadcast_to(gain, (classes, width))
    place = my_place()
    for r in range(devices):
        outs[r][...] = ready[place ^ r]


def pool(vis, fringe, noise, feeds, devices, classes):
    channels, slots, _, skies, lines = vis.shape
    width = slots * skies // devices
    vmem = pl.BlockSpec(memory_space=pltpu.VMEM)
    feeds = feeds.reshape(1, lines)
    return pl.pallas_call(
        functools.partial(pool_kernel, devices, classes),
        in_specs=[pl.BlockSpec(memory_space=pl.ANY)] * 4,
        out_specs=[vmem] * devices,
        out_shape=[jax.ShapeDtypeStruct((3 * classes, width), F32)] * devices,
        scratch_shapes=[
            pltpu.VMEM(vis.shape, BF),
            pltpu.VMEM(fringe.shape, F32),
            pltpu.VMEM(noise.shape, F32),
            pltpu.VMEM(feeds.shape, jnp.int32),
            pltpu.VMEM((devices, 3 * classes, width), F32),
            pltpu.SemaphoreType.DMA((channels,)),
            pltpu.SemaphoreType.DMA((3,)),
        ],
        compiler_params=pltpu.CompilerParams(vmem_limit_bytes=60 << 20),
        cost_estimate=pl.CostEstimate(
            flops=2 * 6 * classes * vis.size, bytes_accessed=2 * vis.size, transcendentals=0
        ),
    )(vis, fringe, noise, feeds)


def near_kernel(sky, beam, held, passed, *outs):
    passed[...] = held[...]
    for i, out in enumerate(outs):
        b_re, b_im = beam[i, 0].astype(F32), beam[i, 1].astype(F32)
        out[...] = dot(rows(b_re, b_im), sky[i, 0], NT) + dot(rows(-b_im, b_re), sky[i, 1], NT)


def near(sky, beam, held):
    each, _, skies, _ = sky.shape
    vmem = pl.BlockSpec(memory_space=pltpu.VMEM)
    return pl.pallas_call(
        near_kernel,
        in_specs=[vmem] * 3,
        out_specs=[vmem] * (each + 1),
        out_shape=[jax.ShapeDtypeStruct(held.shape, F32)]
        + [jax.ShapeDtypeStruct((2 * beam.shape[2], skies), F32)] * each,
        compiler_params=pltpu.CompilerParams(vmem_limit_bytes=8 << 20),
    )(sky, beam, held)


def grad_kernel(cuts, fars, sky, beam, *refs):
    each, _, skies, degrees = sky.shape
    direct, far = refs[:each], refs[each : each + fars]
    pooled = refs[each + fars : -cuts - 1]
    outs, whole = refs[-cuts - 1 : -1], refs[-1]
    classes = beam.shape[2]
    wide = 2 * classes
    step = degrees // cuts
    place = my_place()
    sums = pooled[0][...]
    for ref in pooled[1:]:
        sums = sums + ref[...]
    gain = 0.5 * sums[wide:]
    for i in range(each):
        at = slice(i * skies, (i + 1) * skies)
        parity = jnp.where((place * each + i) % 2 == 0, 1.0, -1.0).astype(F32)
        mine = sky[i]
        if i:
            other = far[0][each - 1 - i + jnp.where(place == 0, 1, 0)]
        else:
            block, blocks = lax.axis_index("ma"), lax.axis_size("ma")
            other = jnp.where((2 * block) % blocks == 0, mine, far[-1][0])
            other = jnp.where(place == 0, other, far[0][each - 1])
        b_re, b_im = beam[i, 0].astype(F32), beam[i, 1].astype(F32)
        crossed = dot(rows(b_re, b_im), other[0], NT) + dot(rows(b_im, -b_re), other[1], NT)
        resp = direct[i][...] + parity * crossed
        p_re = 0.5 * (gain[:, at] * resp[:classes] - sums[:classes, at])
        p_im = 0.5 * (gain[:, at] * resp[classes:] - sums[classes:wide, at])
        own = jnp.concatenate([jnp.concatenate([p_re, p_im], 1), jnp.concatenate([p_im, -p_re], 1)], 0)
        away = parity * jnp.concatenate([jnp.concatenate([p_re, -p_im], 1), jnp.concatenate([p_im, p_re], 1)], 0)
        own = jnp.concatenate(split3(own), 0)
        away = jnp.concatenate(split3(away), 0)
        grad = dot(own, mine.reshape(2 * skies, degrees), NN) + dot(away, other.reshape(2 * skies, degrees), NN)
        grad = grad[:wide] + grad[wide : 2 * wide] + grad[2 * wide :]
        for h in range(cuts):
            whole[h, i] = grad[:, h * step : (h + 1) * step]
    row = lax.axis_index("freq")
    for h in range(cuts):
        outs[h][...] = whole[row ^ h]


def gradient(cuts, sky, beam, direct, far, pooled):
    each = sky.shape[0]
    classes, degrees = beam.shape[2:]
    vmem = pl.BlockSpec(memory_space=pltpu.VMEM)
    shape = (each, 2 * classes, degrees // cuts)
    return pl.pallas_call(
        functools.partial(grad_kernel, cuts, len(far)),
        in_specs=[vmem] * (2 + each + len(far) + len(pooled)),
        out_specs=[vmem] * cuts,
        out_shape=[jax.ShapeDtypeStruct(shape, F32)] * cuts,
        scratch_shapes=[pltpu.VMEM((cuts, *shape), F32)],
        compiler_params=pltpu.CompilerParams(vmem_limit_bytes=8 << 20),
    )(sky, beam, *direct, *far, *pooled)


def join_kernel(*refs):
    pieces, out = refs[:-1], refs[-1]
    each = pieces[0].shape[0]
    place = my_place()
    for r, piece in enumerate(pieces):
        out[pl.ds((place ^ r) * each, each)] = piece[...]


def join(pieces):
    each, wide, step = pieces[0].shape
    vmem = pl.BlockSpec(memory_space=pltpu.VMEM)
    return pl.pallas_call(
        join_kernel,
        in_specs=[vmem] * len(pieces),
        out_specs=vmem,
        out_shape=jax.ShapeDtypeStruct((each * len(pieces), wide, step), F32),
        compiler_params=pltpu.CompilerParams(vmem_limit_bytes=8 << 20),
    )(*pieces)


def body(sky, beam, vis, fringe, noise, feeds):
    slots = sky.shape[0]
    classes = beam.shape[2]
    blocks, cuts, cores = (lax.axis_size(x) for x in ("ma", "freq", "bl"))
    devices = cuts * cores
    each = slots // devices
    place = my_place()

    def across(x, r):
        return lax.ppermute(x, ("freq", "bl"), [(c, c ^ r) for c in range(devices)]) if r else x

    def mirrored(sent, pairs):
        return lax.ppermute(
            sent, ("ma", "freq", "bl"), [(a * devices + c, b * devices + c) for a, b, c in pairs]
        )

    sent = lax.dynamic_slice_in_dim(sky, slots + 1 - (place + 1) * each, each, 0)
    own = lax.dynamic_slice_in_dim(sky, place * each, each, 0)
    own_beam = lax.dynamic_slice_in_dim(beam, place * each, each, 0)
    far = [mirrored(sent, [(a, blocks - 1 - a, c) for a in range(blocks) for c in range(devices)])]
    vis, _ = lax.optimization_barrier((vis, sent))
    sums = pool(vis, fringe, noise, feeds, devices, classes)
    pooled = [across(x, r) for r, x in enumerate(sums)]
    first = lax.optimization_barrier((own, sums[0]))[0][:1]
    far.append(mirrored(first, [(a, blocks - a, 0) for a in range(1, blocks) if 2 * a != blocks]))
    pooled[0], *direct = near(own, own_beam, pooled[0])
    cut = gradient(cuts, own, own_beam, direct, far, pooled)
    cut = [across(x, h * cores) for h, x in enumerate(cut)]
    pieces = [across(x, r) for x in cut for r in range(cores)]
    out = join(pieces)
    return out.reshape(slots, 2, classes, out.shape[-1])


def solution(mesh):
    in_specs = (
        P("ma", None, "grp", None),
        P("ma", None, None, None),
        P("freq", "ma", None, "grp", "bl"),
        P("freq", None, "bl"),
        P("freq", "bl"),
        P("bl"),
    )
    out_specs = P("ma", None, "grp", "freq")
    return jax.shard_map(body, mesh=mesh, in_specs=in_specs, out_specs=out_specs, check_vma=False)
```

```python
import functools

import jax
import jax.numpy as jnp
from jax import lax
from jax.experimental import pallas as pl
from jax.experimental.pallas import tpu as pltpu
from jax.sharding import PartitionSpec as P

BF = jnp.bfloat16
F32 = jnp.float32
AHEAD = 6
NT = (((1,), (1,)), ((), ()))
NN = (((1,), (0,)), ((), ()))


def split3(x):
    top = x.astype(BF)
    rest = x - top.astype(F32)
    mid = rest.astype(BF)
    return top, mid, (rest - mid.astype(F32)).astype(BF)


def dot(a, b, dims):
    return lax.dot_general(a, b, dims, preferred_element_type=F32)


def my_place():
    return lax.axis_index("freq") * lax.axis_size("bl") + lax.axis_index("bl")


def rows(a, b):
    return jnp.concatenate([a, b], 0).astype(BF)


def pool_kernel(devices, classes, vis, fringe, noise, feeds, *refs):
    outs = refs[:devices]
    buf, fringe_v, noise_v, feeds_v, ready, sems, small = refs[devices:]
    channels, slots, _, skies, lines = vis.shape
    ahead = min(AHEAD, channels)
    little = [
        pltpu.make_async_copy(src, dst, small.at[i])
        for i, (src, dst) in enumerate([(feeds, feeds_v), (fringe, fringe_v), (noise, noise_v)])
    ]
    copies = [pltpu.make_async_copy(vis.at[f], buf.at[f], sems.at[f]) for f in range(channels)]
    for copy in little + copies[:ahead]:
        copy.start()
    for copy in little:
        copy.wait()
    onehot = lax.broadcasted_iota(jnp.int32, (classes, lines), 0) == feeds_v[...]
    weight = noise_v[...]
    real = fringe_v[:, 0, :]
    imag = fringe_v[:, 1, :]
    gain = jnp.sum(weight * (real * real + imag * imag), axis=0, keepdims=True)
    gain = jnp.sum(jnp.where(onehot, gain, 0.0), axis=1, keepdims=True)
    parts_re = [p.astype(F32) for p in split3(weight * real)]
    parts_im = [p.astype(F32) for p in split3(-weight * imag)]

    def spread(part, f):
        return jnp.where(onehot, part[f : f + 1, :], 0.0)

    total = None
    for f in range(channels):
        rows_re = [spread(p, f) for p in parts_re]
        rows_im = [spread(p, f) for p in parts_im]
        left_re = jnp.concatenate([y for x in zip(rows_re, rows_im) for y in x], 0).astype(BF)
        left_im = jnp.concatenate([y for x in zip(rows_im, rows_re) for y in (-x[0], x[1])], 0).astype(BF)
        copies[f].wait()
        if f + ahead < channels:
            copies[f + ahead].start()
        for part, left in ((0, left_re), (1, left_im)):
            term = dot(left, buf[f, :, part].reshape(slots * skies, lines), NT)
            total = term if total is None else total + term
    wide = 2 * classes
    total = total[:wide] + total[wide : 2 * wide] + total[2 * wide :]
    width = slots * skies // devices
    for d in range(devices):
        ready[d, :wide] = total[:, d * width : (d + 1) * width]
        ready[d, wide:] = jnp.broadcast_to(gain, (classes, width))
    place = my_place()
    for r in range(devices):
        outs[r][...] = ready[place ^ r]


def pool(vis, fringe, noise, feeds, devices, classes):
    channels, slots, _, skies, lines = vis.shape
    width = slots * skies // devices
    vmem = pl.BlockSpec(memory_space=pltpu.VMEM)
    feeds = feeds.reshape(1, lines)
    return pl.pallas_call(
        functools.partial(pool_kernel, devices, classes),
        in_specs=[pl.BlockSpec(memory_space=pl.ANY)] * 4,
        out_specs=[vmem] * devices,
        out_shape=[jax.ShapeDtypeStruct((3 * classes, width), F32)] * devices,
        scratch_shapes=[
            pltpu.VMEM(vis.shape, BF),
            pltpu.VMEM(fringe.shape, F32),
            pltpu.VMEM(noise.shape, F32),
            pltpu.VMEM(feeds.shape, jnp.int32),
            pltpu.VMEM((devices, 3 * classes, width), F32),
            pltpu.SemaphoreType.DMA((channels,)),
            pltpu.SemaphoreType.DMA((3,)),
        ],
        compiler_params=pltpu.CompilerParams(vmem_limit_bytes=60 << 20),
        cost_estimate=pl.CostEstimate(
            flops=2 * 6 * classes * vis.size, bytes_accessed=2 * vis.size, transcendentals=0
        ),
    )(vis, fringe, noise, feeds)


def hold_kernel(x, out):
    out[...] = x[...]


def hold(x):
    vmem = pl.BlockSpec(memory_space=pltpu.VMEM)
    return pl.pallas_call(
        hold_kernel,
        in_specs=[vmem],
        out_specs=vmem,
        out_shape=jax.ShapeDtypeStruct(x.shape, x.dtype),
        compiler_params=pltpu.CompilerParams(vmem_limit_bytes=8 << 20),
    )(x)


def mirror(far, sky, i):
    each = sky.shape[0]
    first = my_place() == 0
    if i:
        return far[0][each - 1 - i + jnp.where(first, 1, 0)]
    block, blocks = lax.axis_index("ma"), lax.axis_size("ma")
    other = jnp.where((2 * block) % blocks == 0, sky[i], far[1][0])
    return jnp.where(first, other, far[0][each - 1])


def parity_of(slot):
    return jnp.where(slot % 2 == 0, 1.0, -1.0).astype(F32)


def response_kernel(sky, beam, first, second, *outs):
    for i, out in enumerate(outs):
        other = mirror((first, second), sky, i)
        b_re, b_im = beam[i, 0].astype(F32), beam[i, 1].astype(F32)
        direct = dot(rows(b_re, b_im), sky[i, 0], NT) + dot(rows(-b_im, b_re), sky[i, 1], NT)
        crossed = dot(rows(b_re, b_im), other[0], NT) + dot(rows(b_im, -b_re), other[1], NT)
        out[...] = direct + parity_of(my_place() * len(outs) + i) * crossed


def response(sky, beam, far):
    each, _, skies, _ = sky.shape
    vmem = pl.BlockSpec(memory_space=pltpu.VMEM)
    return pl.pallas_call(
        response_kernel,
        in_specs=[vmem] * (2 + len(far)),
        out_specs=[vmem] * each,
        out_shape=[jax.ShapeDtypeStruct((2 * beam.shape[2], skies), F32)] * each,
        compiler_params=pltpu.CompilerParams(vmem_limit_bytes=8 << 20),
    )(sky, beam, *far)


def grad_kernel(cuts, devices, sky, first, second, *refs):
    each, _, skies, degrees = sky.shape
    found, pooled, outs, whole = refs[:each], refs[each : each + devices], refs[each + devices : -1], refs[-1]
    wide = found[0].shape[0]
    classes = wide // 2
    step = degrees // cuts
    sums = functools.reduce(jnp.add, [ref[...] for ref in pooled])
    gain = 0.5 * sums[wide:]
    for i in range(each):
        at = slice(i * skies, (i + 1) * skies)
        parity = parity_of(my_place() * each + i)
        other = mirror((first, second), sky, i)
        resp = found[i][...]
        p_re = 0.5 * (gain[:, at] * resp[:classes] - sums[:classes, at])
        p_im = 0.5 * (gain[:, at] * resp[classes:] - sums[classes:wide, at])
        own = jnp.concatenate([jnp.concatenate([p_re, p_im], 1), jnp.concatenate([p_im, -p_re], 1)], 0)
        away = parity * jnp.concatenate([jnp.concatenate([p_re, -p_im], 1), jnp.concatenate([p_im, p_re], 1)], 0)
        own = jnp.concatenate(split3(own), 0)
        away = jnp.concatenate(split3(away), 0)
        grad = dot(own, sky[i].reshape(2 * skies, degrees), NN) + dot(away, other.reshape(2 * skies, degrees), NN)
        grad = grad[:wide] + grad[wide : 2 * wide] + grad[2 * wide :]
        for h in range(cuts):
            whole[h, i] = grad[:, h * step : (h + 1) * step]
    row = lax.axis_index("freq")
    for h in range(cuts):
        outs[h][...] = whole[row ^ h]


def gradient(cuts, sky, far, found, pooled):
    each, _, _, degrees = sky.shape
    vmem = pl.BlockSpec(memory_space=pltpu.VMEM)
    shape = (each, found[0].shape[0], degrees // cuts)
    return pl.pallas_call(
        functools.partial(grad_kernel, cuts, len(pooled)),
        in_specs=[vmem] * (1 + len(far) + each + len(pooled)),
        out_specs=[vmem] * cuts,
        out_shape=[jax.ShapeDtypeStruct(shape, F32)] * cuts,
        scratch_shapes=[pltpu.VMEM((cuts, *shape), F32)],
        compiler_params=pltpu.CompilerParams(vmem_limit_bytes=8 << 20),
    )(sky, *far, *found, *pooled)


def join_kernel(ranks, *refs):
    pieces, out, sems = refs[: len(ranks)], refs[-2], refs[-1]
    each = pieces[0].shape[0]
    place = my_place()
    copies = [
        pltpu.make_async_copy(piece, out.at[pl.ds((place ^ r) * each, each)], sems.at[n])
        for n, (r, piece) in enumerate(zip(ranks, pieces))
    ]
    for copy in copies:
        copy.start()
    for copy in copies:
        copy.wait()


def join(devices, ranks, pieces, begun=None):
    each, wide, step = pieces[0].shape
    more = [] if begun is None else [begun]
    anywhere = pl.BlockSpec(memory_space=pl.ANY)
    return pl.pallas_call(
        functools.partial(join_kernel, ranks),
        in_specs=[pl.BlockSpec(memory_space=pltpu.VMEM)] * len(pieces) + [anywhere] * len(more),
        out_specs=anywhere,
        out_shape=jax.ShapeDtypeStruct((each * devices, wide, step), F32),
        scratch_shapes=[pltpu.SemaphoreType.DMA((len(pieces),))],
        input_output_aliases={len(pieces): 0} if more else {},
        compiler_params=pltpu.CompilerParams(vmem_limit_bytes=8 << 20),
    )(*pieces, *more)


def body(sky, beam, vis, fringe, noise, feeds):
    slots = sky.shape[0]
    classes = beam.shape[2]
    blocks, cuts, cores = (lax.axis_size(x) for x in ("ma", "freq", "bl"))
    devices = cuts * cores
    each = slots // devices
    place = my_place()

    def across(x, r):
        return lax.ppermute(x, ("freq", "bl"), [(c, c ^ r) for c in range(devices)]) if r else x

    def mirrored(sent, pairs):
        return lax.ppermute(
            sent, ("ma", "freq", "bl"), [(a * devices + c, b * devices + c) for a, b, c in pairs]
        )

    sent = lax.dynamic_slice_in_dim(sky, slots + 1 - (place + 1) * each, each, 0)
    own = lax.dynamic_slice_in_dim(sky, place * each, each, 0)
    own_beam = lax.dynamic_slice_in_dim(beam, place * each, each, 0)
    far = [mirrored(sent, [(a, blocks - 1 - a, c) for a in range(blocks) for c in range(devices)])]
    vis, _ = lax.optimization_barrier((vis, sent))
    sums = pool(vis, fringe, noise, feeds, devices, classes)
    pooled = [across(x, r) for r, x in enumerate(sums)]
    first = lax.optimization_barrier((own, sums[0]))[0][:1]
    far.append(mirrored(first, [(a, blocks - a, 0) for a in range(1, blocks) if 2 * a != blocks]))
    pooled[0] = hold(pooled[0])
    found = response(own, own_beam, far)
    cut = gradient(cuts, own, far, found, pooled)
    cut = [across(x, h * cores) for h, x in enumerate(cut)]
    pieces = [across(x, r) for x in cut for r in range(cores)]
    early = [r for r in range(devices) if r < cores or r % cores == 0]
    late = [r for r in range(devices) if r not in early]
    out = join(devices, early, [pieces[r] for r in early])
    if late:
        out = join(devices, late, [pieces[r] for r in late], out)
    return out.reshape(slots, 2, classes, out.shape[-1])


def solution(mesh):
    in_specs = (
        P("ma", None, "grp", None),
        P("ma", None, None, None),
        P("freq", "ma", None, "grp", "bl"),
        P("freq", None, "bl"),
        P("freq", "bl"),
        P("bl"),
    )
    out_specs = P("ma", None, "grp", "freq")
    return jax.shard_map(body, mesh=mesh, in_specs=in_specs, out_specs=out_specs, check_vma=False)
```

```python
import functools

import jax
import jax.numpy as jnp
from jax import lax
from jax.experimental import pallas as pl
from jax.experimental.pallas import tpu as pltpu
from jax.sharding import PartitionSpec as P

BF = jnp.bfloat16
F32 = jnp.float32
FIRST = 5
AHEAD = 10
NT = (((1,), (1,)), ((), ()))
NN = (((1,), (0,)), ((), ()))


def split3(x):
    top = x.astype(BF)
    rest = x - top.astype(F32)
    mid = rest.astype(BF)
    return top, mid, (rest - mid.astype(F32)).astype(BF)


def dot(a, b, dims):
    return lax.dot_general(a, b, dims, preferred_element_type=F32)


def my_place():
    return lax.axis_index("freq") * lax.axis_size("bl") + lax.axis_index("bl")


def rows(a, b):
    return jnp.concatenate([a, b], 0).astype(BF)


def pool_kernel(devices, classes, vis, fringe, noise, feeds, *refs):
    outs = refs[:devices]
    buf, fringe_v, noise_v, feeds_v, ready, sems, small = refs[devices:]
    channels, slots, _, skies, lines = vis.shape
    ahead = min(AHEAD, channels)
    little = [
        pltpu.make_async_copy(src, dst, small.at[i])
        for i, (src, dst) in enumerate([(feeds, feeds_v), (fringe, fringe_v), (noise, noise_v)])
    ]
    copies = [pltpu.make_async_copy(vis.at[f], buf.at[f], sems.at[f]) for f in range(channels)]
    for copy in little + copies[:FIRST]:
        copy.start()
    for copy in little:
        copy.wait()
    for copy in copies[FIRST:ahead]:
        copy.start()
    onehot = lax.broadcasted_iota(jnp.int32, (classes, lines), 0) == feeds_v[...]
    weight = noise_v[...]
    real = fringe_v[:, 0, :]
    imag = fringe_v[:, 1, :]
    gain = jnp.sum(weight * (real * real + imag * imag), axis=0, keepdims=True)
    gain = jnp.sum(jnp.where(onehot, gain, 0.0), axis=1, keepdims=True)
    parts_re = [p.astype(F32) for p in split3(weight * real)]
    parts_im = [p.astype(F32) for p in split3(-weight * imag)]

    def spread(part, f):
        return jnp.where(onehot, part[f : f + 1, :], 0.0)

    total = None
    for f in range(channels):
        rows_re = [spread(p, f) for p in parts_re]
        rows_im = [spread(p, f) for p in parts_im]
        left_re = jnp.concatenate([y for x in zip(rows_re, rows_im) for y in x], 0).astype(BF)
        left_im = jnp.concatenate([y for x in zip(rows_im, rows_re) for y in (-x[0], x[1])], 0).astype(BF)
        copies[f].wait()
        if f + ahead < channels:
            copies[f + ahead].start()
        for part, left in ((0, left_re), (1, left_im)):
            term = dot(left, buf[f, :, part].reshape(slots * skies, lines), NT)
            total = term if total is None else total + term
    wide = 2 * classes
    total = total[:wide] + total[wide : 2 * wide] + total[2 * wide :]
    width = slots * skies // devices
    for d in range(devices):
        ready[d, :wide] = total[:, d * width : (d + 1) * width]
        ready[d, wide:] = jnp.broadcast_to(gain, (classes, width))
    place = my_place()
    for r in range(devices):
        outs[r][...] = ready[place ^ r]


def pool(vis, fringe, noise, feeds, devices, classes):
    channels, slots, _, skies, lines = vis.shape
    width = slots * skies // devices
    vmem = pl.BlockSpec(memory_space=pltpu.VMEM)
    feeds = feeds.reshape(1, lines)
    return pl.pallas_call(
        functools.partial(pool_kernel, devices, classes),
        in_specs=[pl.BlockSpec(memory_space=pl.ANY)] * 4,
        out_specs=[vmem] * devices,
        out_shape=[jax.ShapeDtypeStruct((3 * classes, width), F32)] * devices,
        scratch_shapes=[
            pltpu.VMEM(vis.shape, BF),
            pltpu.VMEM(fringe.shape, F32),
            pltpu.VMEM(noise.shape, F32),
            pltpu.VMEM(feeds.shape, jnp.int32),
            pltpu.VMEM((devices, 3 * classes, width), F32),
            pltpu.SemaphoreType.DMA((channels,)),
            pltpu.SemaphoreType.DMA((3,)),
        ],
        compiler_params=pltpu.CompilerParams(vmem_limit_bytes=60 << 20),
        cost_estimate=pl.CostEstimate(
            flops=2 * 6 * classes * vis.size, bytes_accessed=2 * vis.size, transcendentals=0
        ),
    )(vis, fringe, noise, feeds)


def hold_kernel(x, out):
    out[...] = x[...]


def hold(x):
    vmem = pl.BlockSpec(memory_space=pltpu.VMEM)
    return pl.pallas_call(
        hold_kernel,
        in_specs=[vmem],
        out_specs=vmem,
        out_shape=jax.ShapeDtypeStruct(x.shape, x.dtype),
        compiler_params=pltpu.CompilerParams(vmem_limit_bytes=8 << 20),
    )(x)


def mirror(far, sky, i):
    each = sky.shape[0]
    first = my_place() == 0
    if i:
        return far[0][each - 1 - i + jnp.where(first, 1, 0)]
    block, blocks = lax.axis_index("ma"), lax.axis_size("ma")
    other = jnp.where((2 * block) % blocks == 0, sky[i], far[1][0])
    return jnp.where(first, other, far[0][each - 1])


def parity_of(slot):
    return jnp.where(slot % 2 == 0, 1.0, -1.0).astype(F32)


def response_kernel(sky, beam, first, second, *outs):
    for i, out in enumerate(outs):
        other = mirror((first, second), sky, i)
        b_re, b_im = beam[i, 0].astype(F32), beam[i, 1].astype(F32)
        direct = dot(rows(b_re, b_im), sky[i, 0], NT) + dot(rows(-b_im, b_re), sky[i, 1], NT)
        crossed = dot(rows(b_re, b_im), other[0], NT) + dot(rows(b_im, -b_re), other[1], NT)
        out[...] = direct + parity_of(my_place() * len(outs) + i) * crossed


def response(sky, beam, far):
    each, _, skies, _ = sky.shape
    vmem = pl.BlockSpec(memory_space=pltpu.VMEM)
    return pl.pallas_call(
        response_kernel,
        in_specs=[vmem] * (2 + len(far)),
        out_specs=[vmem] * each,
        out_shape=[jax.ShapeDtypeStruct((2 * beam.shape[2], skies), F32)] * each,
        compiler_params=pltpu.CompilerParams(vmem_limit_bytes=8 << 20),
    )(sky, beam, *far)


def grad_kernel(cuts, devices, sky, first, second, *refs):
    each, _, skies, degrees = sky.shape
    found, pooled, outs, whole = refs[:each], refs[each : each + devices], refs[each + devices : -1], refs[-1]
    wide = found[0].shape[0]
    classes = wide // 2
    step = degrees // cuts
    sums = functools.reduce(jnp.add, [ref[...] for ref in pooled])
    gain = 0.5 * sums[wide:]
    for i in range(each):
        at = slice(i * skies, (i + 1) * skies)
        parity = parity_of(my_place() * each + i)
        other = mirror((first, second), sky, i)
        resp = found[i][...]
        p_re = 0.5 * (gain[:, at] * resp[:classes] - sums[:classes, at])
        p_im = 0.5 * (gain[:, at] * resp[classes:] - sums[classes:wide, at])
        own = jnp.concatenate([jnp.concatenate([p_re, p_im], 1), jnp.concatenate([p_im, -p_re], 1)], 0)
        away = parity * jnp.concatenate([jnp.concatenate([p_re, -p_im], 1), jnp.concatenate([p_im, p_re], 1)], 0)
        own = jnp.concatenate(split3(own), 0)
        away = jnp.concatenate(split3(away), 0)
        grad = dot(own, sky[i].reshape(2 * skies, degrees), NN) + dot(away, other.reshape(2 * skies, degrees), NN)
        grad = grad[:wide] + grad[wide : 2 * wide] + grad[2 * wide :]
        for h in range(cuts):
            whole[h, i] = grad[:, h * step : (h + 1) * step]
    row = lax.axis_index("freq")
    for h in range(cuts):
        outs[h][...] = whole[row ^ h]


def gradient(cuts, sky, far, found, pooled):
    each, _, _, degrees = sky.shape
    vmem = pl.BlockSpec(memory_space=pltpu.VMEM)
    shape = (each, found[0].shape[0], degrees // cuts)
    return pl.pallas_call(
        functools.partial(grad_kernel, cuts, len(pooled)),
        in_specs=[vmem] * (1 + len(far) + each + len(pooled)),
        out_specs=[vmem] * cuts,
        out_shape=[jax.ShapeDtypeStruct(shape, F32)] * cuts,
        scratch_shapes=[pltpu.VMEM((cuts, *shape), F32)],
        compiler_params=pltpu.CompilerParams(vmem_limit_bytes=8 << 20),
    )(sky, *far, *found, *pooled)


def join_kernel(ranks, *refs):
    pieces, out, sems = refs[: len(ranks)], refs[-2], refs[-1]
    each = pieces[0].shape[0]
    place = my_place()
    copies = [
        pltpu.make_async_copy(piece, out.at[pl.ds((place ^ r) * each, each)], sems.at[n])
        for n, (r, piece) in enumerate(zip(ranks, pieces))
    ]
    for copy in copies:
        copy.start()
    for copy in copies:
        copy.wait()


def join(devices, ranks, pieces, begun=None):
    each, wide, step = pieces[0].shape
    more = [] if begun is None else [begun]
    anywhere = pl.BlockSpec(memory_space=pl.ANY)
    return pl.pallas_call(
        functools.partial(join_kernel, ranks),
        in_specs=[pl.BlockSpec(memory_space=pltpu.VMEM)] * len(pieces) + [anywhere] * len(more),
        out_specs=anywhere,
        out_shape=jax.ShapeDtypeStruct((each * devices, wide, step), F32),
        scratch_shapes=[pltpu.SemaphoreType.DMA((len(pieces),))],
        input_output_aliases={len(pieces): 0} if more else {},
        compiler_params=pltpu.CompilerParams(vmem_limit_bytes=8 << 20),
    )(*pieces, *more)


def body(sky, beam, vis, fringe, noise, feeds):
    slots = sky.shape[0]
    classes = beam.shape[2]
    blocks, cuts, cores = (lax.axis_size(x) for x in ("ma", "freq", "bl"))
    devices = cuts * cores
    each = slots // devices
    place = my_place()

    def across(x, r):
        return lax.ppermute(x, ("freq", "bl"), [(c, c ^ r) for c in range(devices)]) if r else x

    def mirrored(sent, pairs):
        return lax.ppermute(
            sent, ("ma", "freq", "bl"), [(a * devices + c, b * devices + c) for a, b, c in pairs]
        )

    sent = lax.dynamic_slice_in_dim(sky, slots + 1 - (place + 1) * each, each, 0)
    own = lax.dynamic_slice_in_dim(sky, place * each, each, 0)
    own_beam = lax.dynamic_slice_in_dim(beam, place * each, each, 0)
    far = [mirrored(sent, [(a, blocks - 1 - a, c) for a in range(blocks) for c in range(devices)])]
    vis, _ = lax.optimization_barrier((vis, sent))
    sums = pool(vis, fringe, noise, feeds, devices, classes)
    pooled = [across(sums[r], r) for r in sorted(range(devices), key=lambda r: r < cores)]
    first = lax.optimization_barrier((own, sums[0]))[0][:1]
    far.append(mirrored(first, [(a, blocks - a, 0) for a in range(1, blocks) if 2 * a != blocks]))
    at = next(n for n, x in enumerate(pooled) if x is sums[0])
    pooled[at] = hold(sums[0])
    found = response(own, own_beam, far)
    cut = gradient(cuts, own, far, found, pooled)
    cut = [across(x, h * cores) for h, x in enumerate(cut)]
    pieces = [across(x, r) for x in cut for r in range(cores)]
    early = [r for r in range(devices) if r < cores or r % cores == 0]
    late = [r for r in range(devices) if r not in early]
    out = join(devices, early, [pieces[r] for r in early])
    if late:
        out = join(devices, late, [pieces[r] for r in late], out)
    return out.reshape(slots, 2, classes, out.shape[-1])


def solution(mesh):
    in_specs = (
        P("ma", None, "grp", None),
        P("ma", None, None, None),
        P("freq", "ma", None, "grp", "bl"),
        P("freq", None, "bl"),
        P("freq", "bl"),
        P("bl"),
    )
    out_specs = P("ma", None, "grp", "freq")
    return jax.shard_map(body, mesh=mesh, in_specs=in_specs, out_specs=out_specs, check_vma=False)
```

```python
import functools

import jax
import jax.numpy as jnp
from jax import lax
from jax.experimental import pallas as pl
from jax.experimental.pallas import tpu as pltpu
from jax.sharding import PartitionSpec as P

BF = jnp.bfloat16
F32 = jnp.float32
FIRST = 5
AHEAD = 10
NT = (((1,), (1,)), ((), ()))
NN = (((1,), (0,)), ((), ()))


def split3(x):
    top = x.astype(BF)
    rest = x - top.astype(F32)
    mid = rest.astype(BF)
    return top, mid, (rest - mid.astype(F32)).astype(BF)


def dot(a, b, dims):
    return lax.dot_general(a, b, dims, preferred_element_type=F32)


def my_core():
    return lax.axis_index("bl")


def rows(a, b):
    return jnp.concatenate([a, b], 0).astype(BF)


def pool_kernel(cores, classes, vis, fringe, noise, feeds, *refs):
    outs = refs[:cores]
    buf, fringe_v, noise_v, feeds_v, ready, sems, small = refs[cores:]
    channels, slots, _, skies, lines = vis.shape
    ahead = min(AHEAD, channels)
    little = [
        pltpu.make_async_copy(src, dst, small.at[i])
        for i, (src, dst) in enumerate([(feeds, feeds_v), (fringe, fringe_v), (noise, noise_v)])
    ]
    copies = [pltpu.make_async_copy(vis.at[f], buf.at[f], sems.at[f]) for f in range(channels)]
    for copy in little + copies[:FIRST]:
        copy.start()
    for copy in little:
        copy.wait()
    for copy in copies[FIRST:ahead]:
        copy.start()
    onehot = lax.broadcasted_iota(jnp.int32, (classes, lines), 0) == feeds_v[...]
    weight = noise_v[...]
    real = fringe_v[:, 0, :]
    imag = fringe_v[:, 1, :]
    gain = jnp.sum(weight * (real * real + imag * imag), axis=0, keepdims=True)
    gain = jnp.sum(jnp.where(onehot, gain, 0.0), axis=1, keepdims=True)
    parts_re = [p.astype(F32) for p in split3(weight * real)]
    parts_im = [p.astype(F32) for p in split3(-weight * imag)]

    def spread(part, f):
        return jnp.where(onehot, part[f : f + 1, :], 0.0)

    total = None
    for f in range(channels):
        rows_re = [spread(p, f) for p in parts_re]
        rows_im = [spread(p, f) for p in parts_im]
        left_re = jnp.concatenate([y for x in zip(rows_re, rows_im) for y in x], 0).astype(BF)
        left_im = jnp.concatenate([y for x in zip(rows_im, rows_re) for y in (-x[0], x[1])], 0).astype(BF)
        copies[f].wait()
        if f + ahead < channels:
            copies[f + ahead].start()
        for part, left in ((0, left_re), (1, left_im)):
            term = dot(left, buf[f, :, part].reshape(slots * skies, lines), NT)
            total = term if total is None else total + term
    wide = 2 * classes
    total = total[:wide] + total[wide : 2 * wide] + total[2 * wide :]
    width = slots * skies // cores
    for d in range(cores):
        ready[d, :wide] = total[:, d * width : (d + 1) * width]
        ready[d, wide:] = jnp.broadcast_to(gain, (classes, width))
    core = my_core()
    for r in range(cores):
        outs[r][...] = ready[core ^ r]


def pool(vis, fringe, noise, feeds, cores, classes):
    channels, slots, _, skies, lines = vis.shape
    width = slots * skies // cores
    vmem = pl.BlockSpec(memory_space=pltpu.VMEM)
    feeds = feeds.reshape(1, lines)
    return pl.pallas_call(
        functools.partial(pool_kernel, cores, classes),
        in_specs=[pl.BlockSpec(memory_space=pl.ANY)] * 4,
        out_specs=[vmem] * cores,
        out_shape=[jax.ShapeDtypeStruct((3 * classes, width), F32)] * cores,
        scratch_shapes=[
            pltpu.VMEM(vis.shape, BF),
            pltpu.VMEM(fringe.shape, F32),
            pltpu.VMEM(noise.shape, F32),
            pltpu.VMEM(feeds.shape, jnp.int32),
            pltpu.VMEM((cores, 3 * classes, width), F32),
            pltpu.SemaphoreType.DMA((channels,)),
            pltpu.SemaphoreType.DMA((3,)),
        ],
        compiler_params=pltpu.CompilerParams(vmem_limit_bytes=60 << 20),
        cost_estimate=pl.CostEstimate(
            flops=2 * 6 * classes * vis.size, bytes_accessed=2 * vis.size, transcendentals=0
        ),
    )(vis, fringe, noise, feeds)


def hold_kernel(x, out):
    out[...] = x[...]


def hold(x):
    vmem = pl.BlockSpec(memory_space=pltpu.VMEM)
    return pl.pallas_call(
        hold_kernel,
        in_specs=[vmem],
        out_specs=vmem,
        out_shape=jax.ShapeDtypeStruct(x.shape, x.dtype),
        compiler_params=pltpu.CompilerParams(vmem_limit_bytes=8 << 20),
    )(x)


def mirror(far, sky, i):
    each = sky.shape[0]
    first = my_core() == 0
    if i:
        return far[0][each - 1 - i + jnp.where(first, 1, 0)]
    block, blocks = lax.axis_index("ma"), lax.axis_size("ma")
    other = jnp.where((2 * block) % blocks == 0, sky[i], far[1][0])
    return jnp.where(first, other, far[0][each - 1])


def parity_of(slot):
    return jnp.where(slot % 2 == 0, 1.0, -1.0).astype(F32)


def response_kernel(cores, sky, beam, first, second, *refs):
    held, out = refs[:-1], refs[-1]
    each, _, skies, _ = sky.shape
    wide = 2 * beam.shape[2]
    below = out.shape[0] - wide
    out[:below] = functools.reduce(jnp.add, [ref[...] for ref in held])
    for i in range(each):
        other = mirror((first, second), sky, i)
        b_re, b_im = beam[i, 0].astype(F32), beam[i, 1].astype(F32)
        direct = dot(rows(b_re, b_im), sky[i, 0], NT) + dot(rows(-b_im, b_re), sky[i, 1], NT)
        crossed = dot(rows(b_re, b_im), other[0], NT) + dot(rows(b_im, -b_re), other[1], NT)
        out[below:, i * skies : (i + 1) * skies] = direct + parity_of(my_core() * each + i) * crossed


def response(sky, beam, far, held):
    vmem = pl.BlockSpec(memory_space=pltpu.VMEM)
    below, width = held[0].shape
    return pl.pallas_call(
        functools.partial(response_kernel, len(held)),
        in_specs=[vmem] * (2 + len(far) + len(held)),
        out_specs=vmem,
        out_shape=jax.ShapeDtypeStruct((below + 2 * beam.shape[2], width), F32),
        compiler_params=pltpu.CompilerParams(vmem_limit_bytes=8 << 20),
    )(sky, beam, *far, *held)


def grad_kernel(classes, sky, first, second, *refs):
    found, out = refs[:-1], refs[-1]
    each, _, skies, step = sky.shape
    wide = 2 * classes
    sums = functools.reduce(jnp.add, [ref[...] for ref in found])
    gain, resp = 0.5 * sums[wide : 3 * classes], sums[3 * classes :]
    for i in range(each):
        at = slice(i * skies, (i + 1) * skies)
        parity = parity_of(my_core() * each + i)
        other = mirror((first, second), sky, i)
        p_re = 0.5 * (gain[:, at] * resp[:classes, at] - sums[:classes, at])
        p_im = 0.5 * (gain[:, at] * resp[classes:, at] - sums[classes:wide, at])
        own = jnp.concatenate([jnp.concatenate([p_re, p_im], 1), jnp.concatenate([p_im, -p_re], 1)], 0)
        away = parity * jnp.concatenate([jnp.concatenate([p_re, -p_im], 1), jnp.concatenate([p_im, p_re], 1)], 0)
        own = jnp.concatenate(split3(own), 0)
        away = jnp.concatenate(split3(away), 0)
        grad = dot(own, sky[i].reshape(2 * skies, step), NN) + dot(away, other.reshape(2 * skies, step), NN)
        out[i] = grad[:wide] + grad[wide : 2 * wide] + grad[2 * wide :]


def gradient(classes, sky, far, found):
    each, _, _, step = sky.shape
    vmem = pl.BlockSpec(memory_space=pltpu.VMEM)
    return pl.pallas_call(
        functools.partial(grad_kernel, classes),
        in_specs=[vmem] * (1 + len(far) + len(found)),
        out_specs=vmem,
        out_shape=jax.ShapeDtypeStruct((each, 2 * classes, step), F32),
        compiler_params=pltpu.CompilerParams(vmem_limit_bytes=8 << 20),
    )(sky, *far, *found)


def join_kernel(*refs):
    pieces, out, sems = refs[:-2], refs[-2], refs[-1]
    each = pieces[0].shape[0]
    core = my_core()
    copies = [
        pltpu.make_async_copy(piece, out.at[pl.ds((core ^ r) * each, each)], sems.at[r])
        for r, piece in enumerate(pieces)
    ]
    for copy in copies:
        copy.start()
    for copy in copies:
        copy.wait()


def join(pieces):
    each, wide, step = pieces[0].shape
    return pl.pallas_call(
        join_kernel,
        in_specs=[pl.BlockSpec(memory_space=pltpu.VMEM)] * len(pieces),
        out_specs=pl.BlockSpec(memory_space=pl.ANY),
        out_shape=jax.ShapeDtypeStruct((each * len(pieces), wide, step), F32),
        scratch_shapes=[pltpu.SemaphoreType.DMA((len(pieces),))],
        compiler_params=pltpu.CompilerParams(vmem_limit_bytes=8 << 20),
    )(*pieces)


def body(sky, beam, vis, fringe, noise, feeds):
    slots, _, _, degrees = sky.shape
    classes = beam.shape[2]
    blocks, cuts, cores = (lax.axis_size(x) for x in ("ma", "freq", "bl"))
    devices = cuts * cores
    each = slots // cores
    step = degrees // cuts
    core = my_core()
    left = lax.axis_index("freq") * step

    def across(x, r):
        return lax.ppermute(x, ("freq", "bl"), [(c, c ^ r) for c in range(devices)]) if r else x

    def mirrored(sent, pairs):
        return lax.ppermute(
            sent, ("ma", "freq", "bl"), [(a * devices + c, b * devices + c) for a, b, c in pairs]
        )

    def share(x, start):
        return lax.dynamic_slice(x, (start, 0, 0, left), (each, *x.shape[1:3], step))

    sent = share(sky, jnp.minimum(slots + 1 - (core + 1) * each, slots - each))
    own = share(sky, core * each)
    own_beam = share(beam, core * each)
    far = [mirrored(sent, [(a, blocks - 1 - a, c) for a in range(blocks) for c in range(devices)])]
    vis, _ = lax.optimization_barrier((vis, sent))
    sums = pool(vis, fringe, noise, feeds, cores, classes)
    held = [across(x, r) for r, x in enumerate(sums)]
    first = lax.optimization_barrier((own, sums[0]))[0][:1]
    turned = [(a, blocks - a) for a in range(1, blocks) if 2 * a != blocks]
    far.append(mirrored(first, [(a, b, c) for a, b in turned for c in range(0, devices, cores)]))
    held[0] = hold(held[0])
    found = response(own, own_beam, far, held)
    found = [across(found, h * cores) for h in range(cuts)]
    grad = gradient(classes, own, far, found)
    out = join([across(grad, r) for r in range(cores)])
    return out.reshape(slots, 2, classes, step)


def solution(mesh):
    in_specs = (
        P("ma", None, "grp", None),
        P("ma", None, None, None),
        P("freq", "ma", None, "grp", "bl"),
        P("freq", None, "bl"),
        P("freq", "bl"),
        P("bl"),
    )
    out_specs = P("ma", None, "grp", "freq")
    return jax.shard_map(body, mesh=mesh, in_specs=in_specs, out_specs=out_specs, check_vma=False)
```

```python
import functools

import jax
import jax.numpy as jnp
from jax import lax
from jax.experimental import pallas as pl
from jax.experimental.pallas import tpu as pltpu
from jax.sharding import PartitionSpec as P

BF = jnp.bfloat16
F32 = jnp.float32
FIRST = 5
AHEAD = 10
NT = (((1,), (1,)), ((), ()))
NN = (((1,), (0,)), ((), ()))


def split3(x):
    top = x.astype(BF)
    rest = x - top.astype(F32)
    mid = rest.astype(BF)
    return top, mid, (rest - mid.astype(F32)).astype(BF)


def dot(a, b, dims):
    return lax.dot_general(a, b, dims, preferred_element_type=F32)


def my_core():
    return lax.axis_index("bl")


def rows(a, b):
    return jnp.concatenate([a, b], 0).astype(BF)


def pool_kernel(cores, classes, vis, fringe, noise, feeds, *refs):
    outs = refs[:cores]
    buf, fringe_v, noise_v, feeds_v, ready, sems, small = refs[cores:]
    channels, slots, _, skies, lines = vis.shape
    ahead = min(AHEAD, channels)
    little = [
        pltpu.make_async_copy(src, dst, small.at[i])
        for i, (src, dst) in enumerate([(feeds, feeds_v), (fringe, fringe_v), (noise, noise_v)])
    ]
    copies = [pltpu.make_async_copy(vis.at[f], buf.at[f], sems.at[f]) for f in range(channels)]
    for copy in little + copies[:FIRST]:
        copy.start()
    for copy in little:
        copy.wait()
    for copy in copies[FIRST:ahead]:
        copy.start()
    onehot = lax.broadcasted_iota(jnp.int32, (classes, lines), 0) == feeds_v[...]
    weight = noise_v[...]
    real = fringe_v[:, 0, :]
    imag = fringe_v[:, 1, :]
    gain = jnp.sum(weight * (real * real + imag * imag), axis=0, keepdims=True)
    gain = jnp.sum(jnp.where(onehot, gain, 0.0), axis=1, keepdims=True)
    parts_re = [p.astype(F32) for p in split3(weight * real)]
    parts_im = [p.astype(F32) for p in split3(-weight * imag)]

    def spread(part, f):
        return jnp.where(onehot, part[f : f + 1, :], 0.0)

    total = None
    for f in range(channels):
        rows_re = [spread(p, f) for p in parts_re]
        rows_im = [spread(p, f) for p in parts_im]
        left_re = jnp.concatenate([y for x in zip(rows_re, rows_im) for y in x], 0).astype(BF)
        left_im = jnp.concatenate([y for x in zip(rows_im, rows_re) for y in (-x[0], x[1])], 0).astype(BF)
        copies[f].wait()
        if f + ahead < channels:
            copies[f + ahead].start()
        for part, left in ((0, left_re), (1, left_im)):
            term = dot(left, buf[f, :, part].reshape(slots * skies, lines), NT)
            total = term if total is None else total + term
    wide = 2 * classes
    total = total[:wide] + total[wide : 2 * wide] + total[2 * wide :]
    width = slots * skies // cores
    for d in range(cores):
        ready[d, :wide] = total[:, d * width : (d + 1) * width]
        ready[d, wide:] = jnp.broadcast_to(gain, (classes, width))
    core = my_core()
    for r in range(cores):
        outs[r][...] = ready[core ^ r]


def pool(vis, fringe, noise, feeds, cores, classes):
    channels, slots, _, skies, lines = vis.shape
    width = slots * skies // cores
    vmem = pl.BlockSpec(memory_space=pltpu.VMEM)
    feeds = feeds.reshape(1, lines)
    return pl.pallas_call(
        functools.partial(pool_kernel, cores, classes),
        in_specs=[pl.BlockSpec(memory_space=pl.ANY)] * 4,
        out_specs=[vmem] * cores,
        out_shape=[jax.ShapeDtypeStruct((3 * classes, width), F32)] * cores,
        scratch_shapes=[
            pltpu.VMEM(vis.shape, BF),
            pltpu.VMEM(fringe.shape, F32),
            pltpu.VMEM(noise.shape, F32),
            pltpu.VMEM(feeds.shape, jnp.int32),
            pltpu.VMEM((cores, 3 * classes, width), F32),
            pltpu.SemaphoreType.DMA((channels,)),
            pltpu.SemaphoreType.DMA((3,)),
        ],
        compiler_params=pltpu.CompilerParams(vmem_limit_bytes=60 << 20),
        cost_estimate=pl.CostEstimate(
            flops=2 * 6 * classes * vis.size, bytes_accessed=2 * vis.size, transcendentals=0
        ),
    )(vis, fringe, noise, feeds)


def hold_kernel(x, out):
    out[...] = x[...]


def hold(x):
    vmem = pl.BlockSpec(memory_space=pltpu.VMEM)
    return pl.pallas_call(
        hold_kernel,
        in_specs=[vmem],
        out_specs=vmem,
        out_shape=jax.ShapeDtypeStruct(x.shape, x.dtype),
        compiler_params=pltpu.CompilerParams(vmem_limit_bytes=8 << 20),
    )(x)


def mirror(far, sky, i):
    each = sky.shape[0]
    first = my_core() == 0
    if i:
        return far[0][each - 1 - i + jnp.where(first, 1, 0)]
    block, blocks = lax.axis_index("ma"), lax.axis_size("ma")
    other = jnp.where((2 * block) % blocks == 0, sky[i], far[1][0])
    return jnp.where(first, other, far[0][each - 1])


def parity_of(slot):
    return jnp.where(slot % 2 == 0, 1.0, -1.0).astype(F32)


def response_kernel(cores, sky, beam, first, second, *refs):
    held, out = refs[:-1], refs[-1]
    each, _, skies, _ = sky.shape
    wide = 2 * beam.shape[2]
    below = out.shape[0] - wide
    out[:below] = functools.reduce(jnp.add, [ref[...] for ref in held])
    for i in range(each):
        other = mirror((first, second), sky, i)
        b_re, b_im = beam[i, 0].astype(F32), beam[i, 1].astype(F32)
        direct = dot(rows(b_re, b_im), sky[i, 0], NT) + dot(rows(-b_im, b_re), sky[i, 1], NT)
        crossed = dot(rows(b_re, b_im), other[0], NT) + dot(rows(b_im, -b_re), other[1], NT)
        out[below:, i * skies : (i + 1) * skies] = direct + parity_of(my_core() * each + i) * crossed


def response(sky, beam, far, held):
    vmem = pl.BlockSpec(memory_space=pltpu.VMEM)
    below, width = held[0].shape
    return pl.pallas_call(
        functools.partial(response_kernel, len(held)),
        in_specs=[vmem] * (2 + len(far) + len(held)),
        out_specs=vmem,
        out_shape=jax.ShapeDtypeStruct((below + 2 * beam.shape[2], width), F32),
        compiler_params=pltpu.CompilerParams(vmem_limit_bytes=8 << 20),
    )(sky, beam, *far, *held)


def grad_kernel(classes, sky, first, second, *refs):
    found, out = refs[:-1], refs[-1]
    each, _, skies, step = sky.shape
    wide = 2 * classes
    sums = functools.reduce(jnp.add, [ref[...] for ref in found])
    gain, resp = 0.5 * sums[wide : 3 * classes], sums[3 * classes :]
    for i in range(each):
        at = slice(i * skies, (i + 1) * skies)
        parity = parity_of(my_core() * each + i)
        other = mirror((first, second), sky, i)
        p_re = 0.5 * (gain[:, at] * resp[:classes, at] - sums[:classes, at])
        p_im = 0.5 * (gain[:, at] * resp[classes:, at] - sums[classes:wide, at])
        own = jnp.concatenate([jnp.concatenate([p_re, p_im], 1), jnp.concatenate([p_im, -p_re], 1)], 0)
        away = parity * jnp.concatenate([jnp.concatenate([p_re, -p_im], 1), jnp.concatenate([p_im, p_re], 1)], 0)
        own = jnp.concatenate(split3(own), 0)
        away = jnp.concatenate(split3(away), 0)
        grad = dot(own, sky[i].reshape(2 * skies, step), NN) + dot(away, other.reshape(2 * skies, step), NN)
        out[i] = grad[:wide] + grad[wide : 2 * wide] + grad[2 * wide :]


def gradient(classes, sky, far, found):
    each, _, _, step = sky.shape
    vmem = pl.BlockSpec(memory_space=pltpu.VMEM)
    return pl.pallas_call(
        functools.partial(grad_kernel, classes),
        in_specs=[vmem] * (1 + len(far) + len(found)),
        out_specs=vmem,
        out_shape=jax.ShapeDtypeStruct((each, 2 * classes, step), F32),
        compiler_params=pltpu.CompilerParams(vmem_limit_bytes=8 << 20),
    )(sky, *far, *found)


def join_kernel(*refs):
    pieces, out, sems = refs[:-2], refs[-2], refs[-1]
    each = pieces[0].shape[0]
    core = my_core()
    copies = [
        pltpu.make_async_copy(piece, out.at[pl.ds((core ^ r) * each, each)], sems.at[r])
        for r, piece in enumerate(pieces)
    ]
    for copy in copies:
        copy.start()
    for copy in copies:
        copy.wait()


def join(pieces):
    each, wide, step = pieces[0].shape
    return pl.pallas_call(
        join_kernel,
        in_specs=[pl.BlockSpec(memory_space=pltpu.VMEM)] * len(pieces),
        out_specs=pl.BlockSpec(memory_space=pl.ANY),
        out_shape=jax.ShapeDtypeStruct((each * len(pieces), wide, step), F32),
        scratch_shapes=[pltpu.SemaphoreType.DMA((len(pieces),))],
        compiler_params=pltpu.CompilerParams(vmem_limit_bytes=8 << 20),
    )(*pieces)


def body(sky, beam, vis, fringe, noise, feeds):
    slots, _, _, degrees = sky.shape
    classes = beam.shape[2]
    blocks, cuts, cores = (lax.axis_size(x) for x in ("ma", "freq", "bl"))
    devices = cuts * cores
    each = slots // cores
    step = degrees // cuts
    core = my_core()
    left = lax.axis_index("freq") * step

    def across(x, r):
        return lax.ppermute(x, ("freq", "bl"), [(c, c ^ r) for c in range(devices)]) if r else x

    def mirrored(sent, pairs):
        return lax.ppermute(
            sent, ("ma", "freq", "bl"), [(a * devices + c, b * devices + c) for a, b, c in pairs]
        )

    def share(x, start):
        return lax.dynamic_slice(x, (start, 0, 0, left), (each, *x.shape[1:3], step))

    sent = share(sky, jnp.minimum(slots + 1 - (core + 1) * each, slots - each))
    far = [mirrored(sent, [(a, blocks - 1 - a, c) for a in range(blocks) for c in range(devices)])]
    vis, _ = lax.optimization_barrier((vis, sent))
    sums = pool(vis, fringe, noise, feeds, cores, classes)
    held = [across(x, r) for r, x in enumerate(sums)]
    later, later_beam, _ = lax.optimization_barrier((sky, beam, sums[0]))
    own = share(later, core * each)
    own_beam = share(later_beam, core * each)
    first = own[:1]
    turned = [(a, blocks - a) for a in range(1, blocks) if 2 * a != blocks]
    far.append(mirrored(first, [(a, b, c) for a, b in turned for c in range(0, devices, cores)]))
    held[0] = hold(held[0])
    found = response(own, own_beam, far, held)
    found = [across(found, h * cores) for h in range(cuts)]
    grad = gradient(classes, own, far, found)
    out = join([across(grad, r) for r in range(cores)])
    return out.reshape(slots, 2, classes, step)


def solution(mesh):
    in_specs = (
        P("ma", None, "grp", None),
        P("ma", None, None, None),
        P("freq", "ma", None, "grp", "bl"),
        P("freq", None, "bl"),
        P("freq", "bl"),
        P("bl"),
    )
    out_specs = P("ma", None, "grp", "freq")
    return jax.shard_map(body, mesh=mesh, in_specs=in_specs, out_specs=out_specs, check_vma=False)
```

```python
import functools

import jax
import jax.numpy as jnp
from jax import lax
from jax.experimental import pallas as pl
from jax.experimental.pallas import tpu as pltpu
from jax.sharding import PartitionSpec as P

BF = jnp.bfloat16
F32 = jnp.float32
FIRST = 5
AHEAD = 10
NT = (((1,), (1,)), ((), ()))
NN = (((1,), (0,)), ((), ()))


def split3(x):
    top = x.astype(BF)
    rest = x - top.astype(F32)
    mid = rest.astype(BF)
    return top, mid, (rest - mid.astype(F32)).astype(BF)


def dot(a, b, dims):
    return lax.dot_general(a, b, dims, preferred_element_type=F32)


def my_core():
    return lax.axis_index("bl")


def rows(a, b):
    return jnp.concatenate([a, b], 0).astype(BF)


def pool_kernel(cores, classes, vis, fringe, noise, feeds, *refs):
    outs = refs[:cores]
    buf, fringe_v, noise_v, feeds_v, ready, sems, small = refs[cores:]
    channels, slots, _, skies, lines = vis.shape
    ahead = min(AHEAD, channels)
    little = [
        pltpu.make_async_copy(src, dst, small.at[i])
        for i, (src, dst) in enumerate([(feeds, feeds_v), (fringe, fringe_v), (noise, noise_v)])
    ]
    copies = [pltpu.make_async_copy(vis.at[f], buf.at[f], sems.at[f]) for f in range(channels)]
    for copy in little + copies[:FIRST]:
        copy.start()
    for copy in little:
        copy.wait()
    for copy in copies[FIRST:ahead]:
        copy.start()
    onehot = lax.broadcasted_iota(jnp.int32, (classes, lines), 0) == feeds_v[...]
    weight = noise_v[...]
    real = fringe_v[:, 0, :]
    imag = fringe_v[:, 1, :]
    gain = jnp.sum(weight * (real * real + imag * imag), axis=0, keepdims=True)
    gain = jnp.sum(jnp.where(onehot, gain, 0.0), axis=1, keepdims=True)
    parts_re = [p.astype(F32) for p in split3(weight * real)]
    parts_im = [p.astype(F32) for p in split3(-weight * imag)]

    def spread(part, f):
        return jnp.where(onehot, part[f : f + 1, :], 0.0)

    total = None
    for f in range(channels):
        rows_re = [spread(p, f) for p in parts_re]
        rows_im = [spread(p, f) for p in parts_im]
        left_re = jnp.concatenate([y for x in zip(rows_re, rows_im) for y in x], 0).astype(BF)
        left_im = jnp.concatenate([y for x in zip(rows_im, rows_re) for y in (-x[0], x[1])], 0).astype(BF)
        copies[f].wait()
        if f + ahead < channels:
            copies[f + ahead].start()
        for part, left in ((0, left_re), (1, left_im)):
            term = dot(left, buf[f, :, part].reshape(slots * skies, lines), NT)
            total = term if total is None else total + term
    wide = 2 * classes
    total = total[:wide] + total[wide : 2 * wide] + total[2 * wide :]
    width = slots * skies // cores
    for d in range(cores):
        ready[d, :wide] = total[:, d * width : (d + 1) * width]
        ready[d, wide:] = jnp.broadcast_to(gain, (classes, width))
    core = my_core()
    for r in range(cores):
        outs[r][...] = ready[core ^ r]


def pool(vis, fringe, noise, feeds, cores, classes):
    channels, slots, _, skies, lines = vis.shape
    width = slots * skies // cores
    vmem = pl.BlockSpec(memory_space=pltpu.VMEM)
    feeds = feeds.reshape(1, lines)
    return pl.pallas_call(
        functools.partial(pool_kernel, cores, classes),
        in_specs=[pl.BlockSpec(memory_space=pl.ANY)] * 4,
        out_specs=[vmem] * cores,
        out_shape=[jax.ShapeDtypeStruct((3 * classes, width), F32)] * cores,
        scratch_shapes=[
            pltpu.VMEM(vis.shape, BF),
            pltpu.VMEM(fringe.shape, F32),
            pltpu.VMEM(noise.shape, F32),
            pltpu.VMEM(feeds.shape, jnp.int32),
            pltpu.VMEM((cores, 3 * classes, width), F32),
            pltpu.SemaphoreType.DMA((channels,)),
            pltpu.SemaphoreType.DMA((3,)),
        ],
        compiler_params=pltpu.CompilerParams(vmem_limit_bytes=60 << 20),
        cost_estimate=pl.CostEstimate(
            flops=2 * 6 * classes * vis.size, bytes_accessed=2 * vis.size, transcendentals=0
        ),
    )(vis, fringe, noise, feeds)


def hold_kernel(x, out):
    out[...] = x[...]


def hold(x):
    vmem = pl.BlockSpec(memory_space=pltpu.VMEM)
    return pl.pallas_call(
        hold_kernel,
        in_specs=[vmem],
        out_specs=vmem,
        out_shape=jax.ShapeDtypeStruct(x.shape, x.dtype),
        compiler_params=pltpu.CompilerParams(vmem_limit_bytes=8 << 20),
    )(x)


def mirror(far, sky, i):
    each = sky.shape[0]
    first = my_core() == 0
    if i:
        return far[0][each - 1 - i + jnp.where(first, 1, 0)]
    block, blocks = lax.axis_index("ma"), lax.axis_size("ma")
    other = jnp.where((2 * block) % blocks == 0, sky[i], far[1][0])
    return jnp.where(first, other, far[0][each - 1])


def parity_of(slot):
    return jnp.where(slot % 2 == 0, 1.0, -1.0).astype(F32)


def response_kernel(cores, sky, beam, first, second, *refs):
    held, out = refs[:-1], refs[-1]
    each, _, skies, _ = sky.shape
    wide = 2 * beam.shape[2]
    below = out.shape[0] - wide
    out[:below] = functools.reduce(jnp.add, [ref[...] for ref in held])
    for i in range(each):
        other = mirror((first, second), sky, i)
        b_re, b_im = beam[i, 0].astype(F32), beam[i, 1].astype(F32)
        direct = dot(rows(b_re, b_im), sky[i, 0], NT) + dot(rows(-b_im, b_re), sky[i, 1], NT)
        crossed = dot(rows(b_re, b_im), other[0], NT) + dot(rows(b_im, -b_re), other[1], NT)
        out[below:, i * skies : (i + 1) * skies] = direct + parity_of(my_core() * each + i) * crossed


def response(sky, beam, far, held):
    vmem = pl.BlockSpec(memory_space=pltpu.VMEM)
    below, width = held[0].shape
    return pl.pallas_call(
        functools.partial(response_kernel, len(held)),
        in_specs=[vmem] * (2 + len(far) + len(held)),
        out_specs=vmem,
        out_shape=jax.ShapeDtypeStruct((below + 2 * beam.shape[2], width), F32),
        compiler_params=pltpu.CompilerParams(vmem_limit_bytes=8 << 20),
    )(sky, beam, *far, *held)


def grad_kernel(classes, sky, first, second, *refs):
    found, out = refs[:-1], refs[-1]
    each, _, skies, step = sky.shape
    wide = 2 * classes
    sums = functools.reduce(jnp.add, [ref[...] for ref in found])
    gain, resp = 0.5 * sums[wide : 3 * classes], sums[3 * classes :]
    for i in range(each):
        at = slice(i * skies, (i + 1) * skies)
        parity = parity_of(my_core() * each + i)
        other = mirror((first, second), sky, i)
        p_re = 0.5 * (gain[:, at] * resp[:classes, at] - sums[:classes, at])
        p_im = 0.5 * (gain[:, at] * resp[classes:, at] - sums[classes:wide, at])
        own = jnp.concatenate([jnp.concatenate([p_re, p_im], 1), jnp.concatenate([p_im, -p_re], 1)], 0)
        away = parity * jnp.concatenate([jnp.concatenate([p_re, -p_im], 1), jnp.concatenate([p_im, p_re], 1)], 0)
        own = jnp.concatenate(split3(own), 0)
        away = jnp.concatenate(split3(away), 0)
        grad = dot(own, sky[i].reshape(2 * skies, step), NN) + dot(away, other.reshape(2 * skies, step), NN)
        out[i] = grad[:wide] + grad[wide : 2 * wide] + grad[2 * wide :]


def gradient(classes, sky, far, found):
    each, _, _, step = sky.shape
    vmem = pl.BlockSpec(memory_space=pltpu.VMEM)
    return pl.pallas_call(
        functools.partial(grad_kernel, classes),
        in_specs=[vmem] * (1 + len(far) + len(found)),
        out_specs=vmem,
        out_shape=jax.ShapeDtypeStruct((each, 2 * classes, step), F32),
        compiler_params=pltpu.CompilerParams(vmem_limit_bytes=8 << 20),
    )(sky, *far, *found)


def join_kernel(*refs):
    pieces, out, sems = refs[:-2], refs[-2], refs[-1]
    each = pieces[0].shape[0]
    core = my_core()
    copies = [
        pltpu.make_async_copy(piece, out.at[pl.ds((core ^ r) * each, each)], sems.at[r])
        for r, piece in enumerate(pieces)
    ]
    for copy in copies:
        copy.start()
    for copy in copies:
        copy.wait()


def join(pieces):
    each, wide, step = pieces[0].shape
    return pl.pallas_call(
        join_kernel,
        in_specs=[pl.BlockSpec(memory_space=pltpu.VMEM)] * len(pieces),
        out_specs=pl.BlockSpec(memory_space=pl.ANY),
        out_shape=jax.ShapeDtypeStruct((each * len(pieces), wide, step), F32),
        scratch_shapes=[pltpu.SemaphoreType.DMA((len(pieces),))],
        compiler_params=pltpu.CompilerParams(vmem_limit_bytes=8 << 20),
    )(*pieces)


def body(sky, beam, vis, fringe, noise, feeds):
    slots, _, _, degrees = sky.shape
    classes = beam.shape[2]
    blocks, cuts, cores = (lax.axis_size(x) for x in ("ma", "freq", "bl"))
    devices = cuts * cores
    each = slots // cores
    step = degrees // cuts
    core = my_core()
    left = lax.axis_index("freq") * step

    def across(x, r):
        return lax.ppermute(x, ("freq", "bl"), [(c, c ^ r) for c in range(devices)]) if r else x

    def mirrored(sent, pairs):
        return lax.ppermute(
            sent, ("ma", "freq", "bl"), [(a * devices + c, b * devices + c) for a, b, c in pairs]
        )

    def share(x, start):
        return lax.dynamic_slice(x, (start, 0, 0, left), (each, *x.shape[1:3], step))

    sent = share(sky, jnp.minimum(slots + 1 - (core + 1) * each, slots - each))
    own = share(sky, core * each)
    own_beam = share(beam, core * each)
    far = [mirrored(sent, [(a, blocks - 1 - a, c) for a in range(blocks) for c in range(devices)])]
    first = lax.optimization_barrier((own, sent))[0][:1]
    turned = [(a, blocks - a) for a in range(1, blocks) if 2 * a != blocks]
    far.append(mirrored(first, [(a, b, c) for a, b in turned for c in range(0, devices, cores)]))
    vis, _, _ = lax.optimization_barrier((vis, sent, first))
    sums = pool(vis, fringe, noise, feeds, cores, classes)
    held = [across(x, r) for r, x in enumerate(sums)]
    held[0] = hold(held[0])
    found = response(own, own_beam, far, held)
    found = [across(found, h * cores) for h in range(cuts)]
    grad = gradient(classes, own, far, found)
    out = join([across(grad, r) for r in range(cores)])
    return out.reshape(slots, 2, classes, step)


def solution(mesh):
    in_specs = (
        P("ma", None, "grp", None),
        P("ma", None, None, None),
        P("freq", "ma", None, "grp", "bl"),
        P("freq", None, "bl"),
        P("freq", "bl"),
        P("bl"),
    )
    out_specs = P("ma", None, "grp", "freq")
    return jax.shard_map(body, mesh=mesh, in_specs=in_specs, out_specs=out_specs, check_vma=False)
```

```python
import functools

import jax
import jax.numpy as jnp
from jax import lax
from jax.experimental import pallas as pl
from jax.experimental.pallas import tpu as pltpu
from jax.sharding import PartitionSpec as P

BF = jnp.bfloat16
F32 = jnp.float32
FIRST = 5
AHEAD = 10
NT = (((1,), (1,)), ((), ()))
NN = (((1,), (0,)), ((), ()))


def split3(x):
    top = x.astype(BF)
    rest = x - top.astype(F32)
    mid = rest.astype(BF)
    return top, mid, (rest - mid.astype(F32)).astype(BF)


def dot(a, b, dims):
    return lax.dot_general(a, b, dims, preferred_element_type=F32)


def my_core():
    return lax.axis_index("bl")


def rows(a, b):
    return jnp.concatenate([a, b], 0).astype(BF)


def pool_kernel(cores, classes, vis, fringe, noise, feeds, *refs):
    outs = refs[:cores]
    buf, fringe_v, noise_v, feeds_v, ready, sems, small = refs[cores:]
    channels, slots, _, skies, lines = vis.shape
    ahead = min(AHEAD, channels)
    little = [
        pltpu.make_async_copy(src, dst, small.at[i])
        for i, (src, dst) in enumerate([(feeds, feeds_v), (fringe, fringe_v), (noise, noise_v)])
    ]
    copies = [pltpu.make_async_copy(vis.at[f], buf.at[f], sems.at[f]) for f in range(channels)]
    for copy in little + copies[:FIRST]:
        copy.start()
    for copy in little:
        copy.wait()
    for copy in copies[FIRST:ahead]:
        copy.start()
    onehot = lax.broadcasted_iota(jnp.int32, (classes, lines), 0) == feeds_v[...]
    weight = noise_v[...]
    real = fringe_v[:, 0, :]
    imag = fringe_v[:, 1, :]
    gain = jnp.sum(weight * (real * real + imag * imag), axis=0, keepdims=True)
    gain = jnp.sum(jnp.where(onehot, gain, 0.0), axis=1, keepdims=True)
    parts_re = [p.astype(F32) for p in split3(weight * real)]
    parts_im = [p.astype(F32) for p in split3(-weight * imag)]

    def spread(part, f):
        return jnp.where(onehot, part[f : f + 1, :], 0.0)

    total = None
    for f in range(channels):
        rows_re = [spread(p, f) for p in parts_re]
        rows_im = [spread(p, f) for p in parts_im]
        left_re = jnp.concatenate([y for x in zip(rows_re, rows_im) for y in x], 0).astype(BF)
        left_im = jnp.concatenate([y for x in zip(rows_im, rows_re) for y in (-x[0], x[1])], 0).astype(BF)
        copies[f].wait()
        if f + ahead < channels:
            copies[f + ahead].start()
        for part, left in ((0, left_re), (1, left_im)):
            term = dot(left, buf[f, :, part].reshape(slots * skies, lines), NT)
            total = term if total is None else total + term
    wide = 2 * classes
    total = total[:wide] + total[wide : 2 * wide] + total[2 * wide :]
    width = slots * skies // cores
    for d in range(cores):
        ready[d, :wide] = total[:, d * width : (d + 1) * width]
        ready[d, wide:] = jnp.broadcast_to(gain, (classes, width))
    core = my_core()
    for r in range(cores):
        outs[r][...] = ready[core ^ r]


def pool(vis, fringe, noise, feeds, cores, classes):
    channels, slots, _, skies, lines = vis.shape
    width = slots * skies // cores
    vmem = pl.BlockSpec(memory_space=pltpu.VMEM)
    feeds = feeds.reshape(1, lines)
    return pl.pallas_call(
        functools.partial(pool_kernel, cores, classes),
        in_specs=[pl.BlockSpec(memory_space=pl.ANY)] * 4,
        out_specs=[vmem] * cores,
        out_shape=[jax.ShapeDtypeStruct((3 * classes, width), F32)] * cores,
        scratch_shapes=[
            pltpu.VMEM(vis.shape, BF),
            pltpu.VMEM(fringe.shape, F32),
            pltpu.VMEM(noise.shape, F32),
            pltpu.VMEM(feeds.shape, jnp.int32),
            pltpu.VMEM((cores, 3 * classes, width), F32),
            pltpu.SemaphoreType.DMA((channels,)),
            pltpu.SemaphoreType.DMA((3,)),
        ],
        compiler_params=pltpu.CompilerParams(vmem_limit_bytes=60 << 20),
        cost_estimate=pl.CostEstimate(
            flops=2 * 6 * classes * vis.size, bytes_accessed=2 * vis.size, transcendentals=0
        ),
    )(vis, fringe, noise, feeds)


def hold_kernel(x, out):
    out[...] = x[...]


def hold(x):
    vmem = pl.BlockSpec(memory_space=pltpu.VMEM)
    return pl.pallas_call(
        hold_kernel,
        in_specs=[vmem],
        out_specs=vmem,
        out_shape=jax.ShapeDtypeStruct(x.shape, x.dtype),
        compiler_params=pltpu.CompilerParams(vmem_limit_bytes=8 << 20),
    )(x)


def mirror(far, sky, i):
    each = sky.shape[0]
    first = my_core() == 0
    if i:
        return far[0][each - 1 - i + jnp.where(first, 1, 0)]
    block, blocks = lax.axis_index("ma"), lax.axis_size("ma")
    other = jnp.where((2 * block) % blocks == 0, sky[i], far[1][0])
    return jnp.where(first, other, far[0][each - 1])


def parity_of(slot):
    return jnp.where(slot % 2 == 0, 1.0, -1.0).astype(F32)


def response_kernel(cores, sky, beam, first, second, *refs):
    held, out = refs[:-1], refs[-1]
    each, _, skies, _ = sky.shape
    wide = 2 * beam.shape[2]
    below = out.shape[0] - wide
    out[:below] = functools.reduce(jnp.add, [ref[...] for ref in held])
    for i in range(each):
        other = mirror((first, second), sky, i)
        b_re, b_im = beam[i, 0].astype(F32), beam[i, 1].astype(F32)
        direct = dot(rows(b_re, b_im), sky[i, 0], NT) + dot(rows(-b_im, b_re), sky[i, 1], NT)
        crossed = dot(rows(b_re, b_im), other[0], NT) + dot(rows(b_im, -b_re), other[1], NT)
        out[below:, i * skies : (i + 1) * skies] = direct + parity_of(my_core() * each + i) * crossed


def response(sky, beam, far, held):
    vmem = pl.BlockSpec(memory_space=pltpu.VMEM)
    below, width = held[0].shape
    return pl.pallas_call(
        functools.partial(response_kernel, len(held)),
        in_specs=[vmem] * (2 + len(far) + len(held)),
        out_specs=vmem,
        out_shape=jax.ShapeDtypeStruct((below + 2 * beam.shape[2], width), F32),
        compiler_params=pltpu.CompilerParams(vmem_limit_bytes=8 << 20),
    )(sky, beam, *far, *held)


def grad_kernel(classes, sky, first, second, *refs):
    found, out = refs[:-1], refs[-1]
    each, _, skies, step = sky.shape
    wide = 2 * classes
    sums = functools.reduce(jnp.add, [ref[...] for ref in found])
    gain, resp = 0.5 * sums[wide : 3 * classes], sums[3 * classes :]
    for i in range(each):
        at = slice(i * skies, (i + 1) * skies)
        parity = parity_of(my_core() * each + i)
        other = mirror((first, second), sky, i)
        p_re = 0.5 * (gain[:, at] * resp[:classes, at] - sums[:classes, at])
        p_im = 0.5 * (gain[:, at] * resp[classes:, at] - sums[classes:wide, at])
        own = jnp.concatenate([jnp.concatenate([p_re, p_im], 1), jnp.concatenate([p_im, -p_re], 1)], 0)
        away = parity * jnp.concatenate([jnp.concatenate([p_re, -p_im], 1), jnp.concatenate([p_im, p_re], 1)], 0)
        own = jnp.concatenate(split3(own), 0)
        away = jnp.concatenate(split3(away), 0)
        grad = dot(own, sky[i].reshape(2 * skies, step), NN) + dot(away, other.reshape(2 * skies, step), NN)
        out[i] = grad[:wide] + grad[wide : 2 * wide] + grad[2 * wide :]


def gradient(classes, sky, far, found):
    each, _, _, step = sky.shape
    vmem = pl.BlockSpec(memory_space=pltpu.VMEM)
    return pl.pallas_call(
        functools.partial(grad_kernel, classes),
        in_specs=[vmem] * (1 + len(far) + len(found)),
        out_specs=vmem,
        out_shape=jax.ShapeDtypeStruct((each, 2 * classes, step), F32),
        compiler_params=pltpu.CompilerParams(vmem_limit_bytes=8 << 20),
    )(sky, *far, *found)


def join_kernel(ranks, *refs):
    pieces, out, sems = refs[: len(ranks)], refs[-2], refs[-1]
    each = pieces[0].shape[0]
    core = my_core()
    copies = [
        pltpu.make_async_copy(piece, out.at[pl.ds((core ^ r) * each, each)], sems.at[n])
        for n, (r, piece) in enumerate(zip(ranks, pieces))
    ]
    for copy in copies:
        copy.start()
    for copy in copies:
        copy.wait()


def join(cores, ranks, pieces, begun=None):
    each, wide, step = pieces[0].shape
    more = [] if begun is None else [begun]
    anywhere = pl.BlockSpec(memory_space=pl.ANY)
    return pl.pallas_call(
        functools.partial(join_kernel, ranks),
        in_specs=[pl.BlockSpec(memory_space=pltpu.VMEM)] * len(pieces) + [anywhere] * len(more),
        out_specs=anywhere,
        out_shape=jax.ShapeDtypeStruct((each * cores, wide, step), F32),
        scratch_shapes=[pltpu.SemaphoreType.DMA((len(pieces),))],
        input_output_aliases={len(pieces): 0} if more else {},
        compiler_params=pltpu.CompilerParams(vmem_limit_bytes=8 << 20),
    )(*pieces, *more)


def body(sky, beam, vis, fringe, noise, feeds):
    slots, _, _, degrees = sky.shape
    classes = beam.shape[2]
    blocks, cuts, cores = (lax.axis_size(x) for x in ("ma", "freq", "bl"))
    devices = cuts * cores
    each = slots // cores
    step = degrees // cuts
    core = my_core()
    left = lax.axis_index("freq") * step

    def across(x, r):
        return lax.ppermute(x, ("freq", "bl"), [(c, c ^ r) for c in range(devices)]) if r else x

    def mirrored(sent, pairs):
        return lax.ppermute(
            sent, ("ma", "freq", "bl"), [(a * devices + c, b * devices + c) for a, b, c in pairs]
        )

    def share(x, start):
        return lax.dynamic_slice(x, (start, 0, 0, left), (each, *x.shape[1:3], step))

    sent = share(sky, jnp.minimum(slots + 1 - (core + 1) * each, slots - each))
    own = share(sky, core * each)
    own_beam = share(beam, core * each)
    far = [mirrored(sent, [(a, blocks - 1 - a, c) for a in range(blocks) for c in range(devices)])]
    vis, _ = lax.optimization_barrier((vis, sent))
    sums = pool(vis, fringe, noise, feeds, cores, classes)
    held = [across(x, r) for r, x in enumerate(sums)]
    first = lax.optimization_barrier((own, sums[0]))[0][:1]
    turned = [(a, blocks - a) for a in range(1, blocks) if 2 * a != blocks]
    far.append(mirrored(first, [(a, b, c) for a, b in turned for c in range(0, devices, cores)]))
    held[0] = hold(held[0])
    found = response(own, own_beam, far, held)
    found = [across(found, h * cores) for h in range(cuts)]
    grad = gradient(classes, own, far, found)
    out = join(cores, [0], [grad])
    if cores > 1:
        out = join(cores, list(range(1, cores)), [across(grad, r) for r in range(1, cores)], out)
    return out.reshape(slots, 2, classes, step)


def solution(mesh):
    in_specs = (
        P("ma", None, "grp", None),
        P("ma", None, None, None),
        P("freq", "ma", None, "grp", "bl"),
        P("freq", None, "bl"),
        P("freq", "bl"),
        P("bl"),
    )
    out_specs = P("ma", None, "grp", "freq")
    return jax.shard_map(body, mesh=mesh, in_specs=in_specs, out_specs=out_specs, check_vma=False)
```
